128 devices in a mesh: wide: 16 (over z, x), narrow: 8 (over y, core).
Axes of the slice: x: 4, y: 4, z: 4, core: 2. Of those that a mesh axis runs over, the one named last changes fastest.
Arguments:
- samples: bfloat16 [16, 4096, 48, 128], P('wide', 'narrow'), may hold values from -6 to 6
- spacing: bfloat16 [16, 4096, 48], P('wide', 'narrow'), may hold values from 0.00019931793 to 0.0049743652
- region_ids: int32 [16, 4096, 1], P('wide', 'narrow'), may hold values from 0 to 511; in each aligned block of 512 rows (0 to 511, 512 to 1023, ..., all dimensions but the last counted through in order) at most 2 rows name the same one
- directions: int32 [4096], P('narrow'), may hold values 0 or 1
- w_in: bfloat16 [512, 128, 256], P(('wide', 'narrow')), may hold values from -0.75 to 0.75
- w_mid: bfloat16 [512, 2, 256, 256], P(('wide', 'narrow')), may hold values from -0.5 to 0.5
- w_out: bfloat16 [512, 4, 256], P(('wide', 'narrow')), may hold values from -0.75 to 0.75
Outputs:
- ray_colour: float32 [3, 4096], P(None, 'narrow')
The draws below stay inside these ranges and needn't reach their ends.
Inputs may be any that keep to these rules, and one draw needn't show every extreme that they name: `region_ids`: among the 512 segments of one device (aligned blocks of rows of the flattened first two dimensions) at most 2 name any one region, a bound that some block reaches there.
All inputs are finite; a program needn't handle non-finite values. No bound on the sum of `directions` on one device may be relied on, other than what follows from the above.
Results may differ from the reference program's by a relative error of at most 0.00058.
Values may be sent and summed in bfloat16 or wider, within the bound.
A program may use at most 128 MiB of HBM per device.

```python
import math
import jax
import jax.numpy as jnp
import numpy as np
from jax import lax

H = 256
F_IN = 128
MID = 2
SAMPLES = 48
RAY_DEV = 512
SEGS = 16
RAYS = 4096
REGIONS = 512
MOST = 2
DEVICES = 128


def plant(drawn, rng, low, top_value):
    longest = drawn.shape.index(max(drawn.shape))
    spots = []
    for shift in (0, 1):
        where = [jax.random.randint(jax.random.fold_in(rng, axis), (), 0, length) for axis, length in enumerate(drawn.shape)]
        where[longest] = (where[longest] + shift) % drawn.shape[longest]
        spots.append(tuple(where))
    return drawn.at[spots[0]].set(low).at[spots[1]].set(top_value)


def block_scale(rng, dims, pieces, smallest, high):
    gain = 1.0
    for dim, blocks in pieces:
        steps = jax.random.uniform(jax.random.fold_in(jax.random.fold_in(rng, 6), dim), (blocks,), jnp.float32, smallest / len(pieces), high / len(pieces))
        gain = gain * jnp.repeat(jnp.exp(steps), dims[dim] // blocks).reshape((-1,) + (1,) * (len(dims) - 1 - dim))
    return gain


def assign_block(stream_key, own, number, rows, count, top, bound, skew):
    sequence = jax.random.permutation(stream_key, count)
    heavy_load, common = load_shares(count, rows * top, bound, skew, True), load_shares(count, rows * top, bound, skew, False)
    places = jnp.arange(count)

    def named(sizes, offset_by):
        used = int((sizes > 0).sum())
        fixed = max(1, used // 4)
        shifted = fixed + (places - fixed + offset_by * (used - fixed)) % max(1, count - fixed)
        return jnp.zeros((count,), jnp.int32).at[sequence[jnp.where(places < fixed, places, shifted)]].set(jnp.asarray(sizes, jnp.int32))

    sizes = jnp.where(number % 4 == 0, named(heavy_load, number // 4), named(common, number - number // 4 - 1))
    mixed = jax.random.permutation(jax.random.fold_in(own, 3), count)
    source_of, receiver = mixed[0:count // 2 * 2:2], mixed[1:count // 2 * 2:2]
    slack = jnp.minimum(sizes[source_of] - 1, bound - sizes[receiver]) // 2
    slack = jnp.where((source_of == sequence[0]) | (receiver == sequence[0]) | (sizes[receiver] == 0), 0, jnp.maximum(slack, 0))
    shifted = jax.random.randint(jax.random.fold_in(own, 4), (count // 2,), 0, 1 << 20) % (slack + 1)
    sizes = sizes.at[source_of].add(-shifted).at[receiver].add(shifted)
    labels = jnp.searchsorted(jnp.cumsum(sizes), jnp.arange(rows * top), side="right").astype(jnp.int32)
    grid = labels.reshape(top, rows).T
    grid = grid[jax.random.permutation(jax.random.fold_in(own, 1), rows)]
    offset_by = jax.random.randint(jax.random.fold_in(own, 2), (rows, 1), 0, top)
    return jnp.take_along_axis(grid, (jnp.arange(top)[None, :] + offset_by) % top, axis=1)


def load_shares(count, total, most, skew, full):
    weights = [(1 << 20) // math.isqrt(grade ** skew) + 1 for grade in range(1, count + 1)]
    largest = most if full else min(most, max(-(-total // count), total * weights[0] // sum(weights)))
    least = 1 if total - largest >= count - 1 else 0
    given, rest = [largest] + [least] * (count - 1), total - largest - least * (count - 1)
    while rest > 0:
        free = [i for i in range(1, count) if given[i] < largest] or [i for i in range(1, count) if given[i] < most]
        pool, budget = sum([weights[i] for i in free]), rest
        for i in free:
            addition = min(most - given[i], max(1, budget * weights[i] // pool), rest)
            given[i] = given[i] + addition
            rest = rest - addition
    return np.array(given)


def bell_draw(stream_key, extent, spread, bound, split=(), held_as=jnp.bfloat16):
    array = jax.random.normal(stream_key, extent, jnp.float32) * spread
    if len(split) > 0:
        array = block_scale(stream_key, extent, split, -0.22, 0.18) * array
    return jnp.clip(array, min=-bound, max=bound).astype(held_as)


def setup_inputs(seed: int = 0) -> dict:
    streams_of = jax.random.split(jax.random.key(seed), 8)
    samples = bell_draw(streams_of[0], (SEGS, RAYS, SAMPLES, F_IN), 1.0, 6.0, ((0, 16), (1, 8)))
    spacing = jnp.clip(jnp.exp(math.log(0.0049743652) - 3.2171519 * jax.random.uniform(streams_of[1], (SEGS, RAYS, SAMPLES), jnp.float32) ** block_scale(streams_of[1], (SEGS, RAYS, SAMPLES), ((0, 16), (1, 8)), -0.2, 0.2)), 0.00019931793, 0.0049743652).astype(jnp.bfloat16)
    region_ids_keys = jax.random.split(jax.random.fold_in(streams_of[2], 1), SEGS * RAYS // RAY_DEV)
    region_ids_turns = jax.random.permutation(jax.random.fold_in(streams_of[2], 3), SEGS * RAYS // RAY_DEV)
    region_ids = jax.vmap(lambda own, number: assign_block(jax.random.fold_in(streams_of[2], 2), own, number, RAY_DEV, REGIONS, 1, MOST, 2))(region_ids_keys, region_ids_turns).reshape((SEGS, RAYS, 1))
    directions = plant((jax.random.randint(streams_of[3], (RAYS,), 0, 2) < 1).astype(jnp.int32), jax.random.fold_in(streams_of[3], 1), 0, 1)
    w_in = bell_draw(streams_of[4], (REGIONS, F_IN, H), (F_IN // 2) ** -0.5, 0.75, ((0, 128),))
    w_mid = bell_draw(streams_of[5], (REGIONS, MID, H, H), (H // 2) ** -0.5, 0.5, ((0, 128),))
    w_out = bell_draw(streams_of[6], (REGIONS, 4, H), (H // 4) ** -0.5, 0.75, ((0, 128),))
    return dict(samples=samples, spacing=spacing, region_ids=region_ids, directions=directions, w_in=w_in, w_mid=w_mid, w_out=w_out)


def composite(raw_out, spacing_part):
    density = jax.nn.softplus(raw_out[0])
    colours = jax.nn.sigmoid(raw_out[1:4])
    optical = density * spacing_part.astype(jnp.float32)
    before_sum = jnp.cumsum(optical, axis=-1) - optical
    sample_weight = jnp.exp(-before_sum) * (-jnp.expm1(-optical))
    seg_colour = jnp.sum(sample_weight * colours, axis=-1)
    seg_depth = jnp.sum(optical, axis=-1)
    return jnp.stack([seg_colour[0], seg_colour[1], seg_colour[2], seg_depth], axis=-1)


def region_partials(features, spacing_part, first_w, inner_w, head_w):
    inputs = features.reshape(-1, F_IN)
    hidden = jax.nn.relu(jnp.dot(inputs, first_w, preferred_element_type=jnp.float32)).astype(jnp.bfloat16)
    for layer_index in range(MID):
        hidden = jax.nn.relu(jnp.dot(hidden, inner_w[layer_index], preferred_element_type=jnp.float32)).astype(jnp.bfloat16)
    raw_out = jnp.einsum("nh,ch->cn", hidden.astype(jnp.float32), head_w.astype(jnp.float32))
    raw_out = raw_out.reshape(4, features.shape[0], SAMPLES)
    return composite(raw_out, spacing_part)


def reference(samples, spacing, region_ids, directions, w_in, w_mid, w_out):
    seg_total = SEGS * RAYS
    flat_features = samples.reshape(seg_total, SAMPLES, F_IN)
    flat_spacing = spacing.reshape(seg_total, SAMPLES)
    region_row = region_ids.reshape(seg_total)
    capacity = MOST * DEVICES

    def one_region(region):
        picked = jnp.nonzero(region_row == region, size=capacity, fill_value=seg_total)[0].astype(jnp.int32)
        features = jnp.take(flat_features, picked, axis=0, mode="clip")
        spacing_part = jnp.take(flat_spacing, picked, axis=0, mode="clip")
        values_out = region_partials(features, spacing_part, w_in[region], w_mid[region], w_out[region])
        return picked, values_out

    picked, values_out = lax.map(one_region, jnp.arange(REGIONS, dtype=jnp.int32))
    partial_value = jnp.zeros((seg_total, 4), jnp.float32).at[picked.reshape(-1)].set(values_out.reshape(-1, 4), mode="drop")
    partial_value = partial_value.reshape(SEGS, RAYS, 4)
    seg_depth = partial_value[..., 3]
    running = jnp.cumsum(seg_depth, axis=0)
    ahead = running - seg_depth
    behind = running[-1][None, :] - running
    prefix = jnp.where(directions[None, :] == 1, behind, ahead)
    light = jnp.exp(-prefix)
    return jnp.sum(light[..., None] * partial_value[..., :3], axis=0).T
```

```python
import jax
import jax.numpy as jnp
from jax import lax
from jax.experimental import pallas as pl
from jax.experimental.pallas import tpu as pltpu
from jax.sharding import PartitionSpec as P

MESH = pl.DeviceIdType.MESH
F32, BF16, I32 = jnp.float32, jnp.bfloat16, jnp.int32
ROWS, SAMP, FEAT, HID = 512, 48, 128, 256
WIDE, NARROW, REG, GROUP = 16, 8, 4, 32
CAP = 40
PIECE = 8
META = 48
FLAG = 127

SEND_ORDER = ((6, 14, 9, 11, 1, 3, 4, 12, 2, 8, 10), (5, 15, 7, 13))
CHUNKS = ((0, 6, 14, 9), (11, 1, 3, 4), (12, 2, 8, 10), (5, 15, 7, 13))
DY_ORDER = (1, 3, 2)


def nt(a, b, precision=None):
    return lax.dot_general(a, b, (((1,), (1,)), ((), ())), precision=precision, preferred_element_type=F32)


def tn(a, b, precision=None):
    return lax.dot_general(a, b, (((0,), (0,)), ((), ())), precision=precision, preferred_element_type=F32)


def dot(a, b, precision=None):
    return jnp.dot(a, b, precision=precision, preferred_element_type=F32)


def onehot(rows, lanes_value):
    return lax.broadcasted_iota(I32, (rows, lanes_value.shape[1]), 0) == lanes_value


def within(i, size):
    return jnp.minimum(jnp.maximum(i, 0), size - 1)


def relu(v):
    return jnp.maximum(v.astype(BF16), 0)


def prefix_2(array, axis, combine, identity, reverse):
    count, position = (lax.axis_size(axis), lax.axis_index(axis))
    everything = lax.all_gather(array, axis)
    start = jnp.broadcast_to(jnp.asarray(identity, array.dtype), array.shape)

    def hop(k, before):
        at = count - 1 - k if reverse else k
        reached = at > position if reverse else at < position
        new = combine(before, everything[at])
        return jnp.where(reached, new, before)

    return lax.fori_loop(0, count, hop, start)


def composite(raw_out, spacing_part):
    density = jax.nn.softplus(raw_out[0])
    colours = jax.nn.sigmoid(raw_out[1:4])
    optical = density * spacing_part.astype(jnp.float32)
    before_sum = jnp.cumsum(optical, axis=-1) - optical
    sample_weight = jnp.exp(-before_sum) * -jnp.expm1(-optical)
    seg_colour = jnp.sum(sample_weight * colours, axis=-1)
    seg_depth = jnp.sum(optical, axis=-1)
    return jnp.stack([seg_colour[0], seg_colour[1], seg_colour[2], seg_depth], axis=-1)


def accumulate(earlier, later):
    return earlier + later


def general(samples, spacing, region_ids, directions, w_in, w_mid, w_out):
    wide_size = lax.axis_size("wide")
    narrow_size = lax.axis_size("narrow")
    devices_all = wide_size * narrow_size
    reg_local = w_in.shape[0]
    ray_local = samples.shape[1]
    sample_len = samples.shape[2]
    width_in = samples.shape[3]
    region_all = reg_local * devices_all
    capacity = max(2, 2 * ray_local // region_all)
    slot_total = region_all * capacity
    region_row = region_ids.reshape(ray_local)
    matches = region_row[:, None] == region_row[None, :]
    positions = jnp.arange(ray_local, dtype=jnp.int32)
    earlier = positions[None, :] < positions[:, None]
    arrival = jnp.sum(jnp.logical_and(matches, earlier), axis=1)
    slot_index = region_row * capacity + arrival
    source_row = jnp.full((slot_total,), ray_local, jnp.int32).at[slot_index].set(positions)
    ray_rows = jnp.concatenate(
        [
            samples.reshape(ray_local, sample_len, width_in),
            jnp.zeros((1, sample_len, width_in), samples.dtype),
        ],
        axis=0,
    )
    gap_rows = jnp.concatenate(
        [spacing.reshape(ray_local, sample_len), jnp.zeros((1, sample_len), spacing.dtype)], axis=0
    )
    send_features = jnp.take(ray_rows, source_row, axis=0)
    send_spacing = jnp.take(gap_rows, source_row, axis=0)
    features = lax.all_to_all(
        send_features.reshape(devices_all, reg_local, capacity, sample_len, width_in),
        ("wide", "narrow"),
        split_axis=0,
        concat_axis=0,
        tiled=True,
    )
    spacing_part = lax.all_to_all(
        send_spacing.reshape(devices_all, reg_local, capacity, sample_len),
        ("wide", "narrow"),
        split_axis=0,
        concat_axis=0,
        tiled=True,
    )
    results = []
    for region in range(reg_local):
        inputs = features[:, region].reshape(-1, width_in)
        hidden = jax.nn.relu(
            jnp.dot(inputs, w_in[region], preferred_element_type=jnp.float32)
        ).astype(jnp.bfloat16)
        for layer_index in range(w_mid.shape[1]):
            hidden = jax.nn.relu(
                jnp.dot(hidden, w_mid[region, layer_index], preferred_element_type=jnp.float32)
            ).astype(jnp.bfloat16)
        raw_out = jnp.einsum("nh,ch->cn", hidden, w_out[region], preferred_element_type=jnp.float32)
        part_gap = spacing_part[:, region]
        raw_out = raw_out.reshape((4,) + part_gap.shape)
        results.append(composite(raw_out, part_gap))
    partial_here = jnp.stack(results, axis=1)
    returned = lax.all_to_all(
        partial_here, ("wide", "narrow"), split_axis=0, concat_axis=0, tiled=True
    )
    mine = jnp.take(returned.reshape(slot_total, 4), slot_index, axis=0)
    seg_depth = mine[:, 3]
    zero_depth = jnp.zeros_like(seg_depth)
    ahead = prefix_2(seg_depth, "wide", accumulate, zero_depth, False)
    behind = prefix_2(seg_depth, "wide", accumulate, zero_depth, True)
    prefix = jnp.where(directions == 1, behind, ahead)
    light = jnp.exp(-prefix)
    light_term = (light[:, None] * mine[:, :3]).T
    return lax.psum(light_term, "wide")


def render_kernel(samples, spacing, ids, dirs, w_in, w_mid, w_out, out, *scratch):
    (rows, send, recv0, recv1, recv2, recv3, wi, wm, wo, wp, meta_s, meta_r, pos_v, pos_s, idx_v, idx_s, acc,
     ret_s, ret_r, fin_s, fin_r, flag_s, flag_r, local_sem, wt_send, wt_recv, fwd_send, meta_ss, meta_rs,
     data_ss, data_rs, ret_ss, ret_rs, fin_ss, fin_rs, flag_ss, flag_rs) = scratch
    recv = (recv0, recv1, recv2, recv3)
    place = {k: (q, s) for q, chunk in enumerate(CHUNKS) for s, k in enumerate(chunk)}
    wide, nar = lax.axis_index("wide"), lax.axis_index("narrow")
    z, x = wide // 4, wide % 4
    y, core = nar // 2, nar % 2

    def group_at(k, sign=1):
        return ((z + sign * (k // 4) + 4) % 4) * 4 + (x + sign * (k % 4) + 4) % 4

    def wide_at(k, sign=1):
        return (group_at(k, sign), nar)

    def narrow_at(dy, dc, sign=1):
        return (wide, ((y + sign * dy + 4) % 4) * 2 + (core + dc) % 2)

    def remote(src, dst, ss, rs, to):
        return pltpu.make_async_remote_copy(
            src_ref=src, dst_ref=dst, send_sem=ss, recv_sem=rs, device_id=to, device_id_type=MESH)

    barrier = pltpu.get_barrier_semaphore()
    for k in range(1, WIDE):
        pl.semaphore_signal(barrier, inc=1, device_id=wide_at(k), device_id_type=MESH)
    for t in range(1, NARROW):
        pl.semaphore_signal(barrier, inc=1, device_id=narrow_at(t // 2, t % 2), device_id_type=MESH)

    here = [pltpu.make_async_copy(samples, rows, local_sem.at[0]),
            pltpu.make_async_copy(w_in, wi.at[pl.ds(0, REG)], local_sem.at[1]),
            pltpu.make_async_copy(w_mid, wm.at[pl.ds(0, REG)], local_sem.at[2]),
            pltpu.make_async_copy(w_out, wo.at[0], local_sem.at[3])]
    for copy in here:
        copy.start()

    rid = ids[...]
    g = jnp.right_shift(rid, 5)
    nb = jnp.bitwise_and(jnp.right_shift(rid, 2), 7)
    t = jnp.bitwise_and(jnp.right_shift(nb, 1) - y, 3) * 2 + jnp.bitwise_and(nb + core, 1)
    r = t * REG + jnp.bitwise_and(rid, 3)
    ray = lax.broadcasted_iota(I32, (1, ROWS), 1)
    before = (lax.broadcasted_iota(I32, (ROWS, ROWS), 0) < lax.broadcasted_iota(I32, (ROWS, ROWS), 1)).astype(BF16)
    of_region = onehot(WIDE * GROUP, g * GROUP + r).astype(F32)
    a = jnp.sum(of_region * dot(of_region.astype(BF16), before), axis=0, keepdims=True)
    of_group = onehot(WIDE, g).astype(F32)
    p = jnp.sum(of_group * dot(of_group.astype(BF16), before), axis=0, keepdims=True)
    a_int, p_int = a.astype(I32), p.astype(I32)
    at_place = onehot(128, p_int).astype(BF16)
    low = nt((of_group * jnp.bitwise_and(ray, 15).astype(F32)).astype(BF16), at_place)
    high = nt((of_group * jnp.right_shift(ray, 4).astype(F32)).astype(BF16), at_place)
    idx_v[...] = (low + 16.0 * high).astype(I32)
    to_smem = pltpu.make_async_copy(idx_v, idx_s, local_sem.at[4])
    to_smem.start()
    slot = onehot(128, a_int * GROUP + r).astype(BF16)
    position = nt((of_group * jnp.minimum(p, CAP - 1.0)).astype(BF16), slot)
    over = (jnp.max(p, axis=1, keepdims=True) >= CAP).astype(F32)
    position = jnp.where(lax.broadcasted_iota(I32, (WIDE, 128), 1) == FLAG, over, position)
    lane = lax.broadcasted_iota(I32, (SAMP, 128), 1)
    samp = lax.broadcasted_iota(I32, (SAMP, 128), 0)
    gaps = spacing[...]
    first = dot(gaps, (lane == samp).astype(BF16)).astype(BF16)
    second = dot(gaps, (lane == samp + SAMP).astype(BF16)).astype(BF16)
    gap_slots = dot((of_region * (1.0 - a)).astype(BF16), first) + dot((of_region * a).astype(BF16), second)
    meta_s[:, 0:GROUP, :] = gap_slots.astype(BF16).reshape(WIDE, GROUP, 128)
    for w in range(WIDE):
        meta_s[w, GROUP:META, :] = jnp.broadcast_to(position[w:w + 1], (META - GROUP, 128)).astype(BF16)
    meta_r[0] = meta_s[wide]

    pl.semaphore_wait(barrier, WIDE - 1 + NARROW - 1)

    def weight_copies(s, to, mine):
        source = (w_in, w_mid, w_out) if mine else (
            wi.at[pl.ds((s - 1) * REG, REG)], wm.at[pl.ds((s - 1) * REG, REG)], wo.at[s - 1])
        target = (wi.at[pl.ds(s * REG, REG)], wm.at[pl.ds(s * REG, REG)], wo.at[s])
        return [remote(source[i], target[i], wt_send.at[i, s], wt_recv.at[i, s], to) for i in range(3)]

    weights = {1: weight_copies(1, narrow_at(0, 1), True)}
    for dy in DY_ORDER:
        weights[2 * dy] = weight_copies(2 * dy, narrow_at(dy, 0, -1), True)
        weights[2 * dy + 1] = weight_copies(2 * dy + 1, narrow_at(0, 1), False)
    for s in (1,) + tuple(2 * dy for dy in DY_ORDER):
        for copy in weights[s]:
            copy.start()

    metas = {k: remote(meta_s.at[group_at(k)], meta_r.at[k], meta_ss.at[k], meta_rs.at[k], wide_at(k))
             for order in SEND_ORDER for k in order}
    for copy in metas.values():
        copy.start()

    here[0].wait()
    to_smem.wait()

    def data_copy(k, start, size):
        q, s = place[k]
        return remote(send.at[k - 1, pl.ds(start, size)], recv[q].at[pl.ds(s * CAP + start, size)],
                      data_ss.at[k], data_rs.at[k], wide_at(k))

    for order in SEND_ORDER:
        def pack(piece, carry, order=order):
            for k in order:
                to = group_at(k)
                for m in range(PIECE):
                    send[k - 1, piece * PIECE + m] = rows[within(idx_s[to, piece * PIECE + m], ROWS)]
                data_copy(k, piece * PIECE, PIECE).start()
            return carry

        lax.fori_loop(0, CAP // PIECE, pack, 0)

    def pack_own(piece, carry):
        q, s = place[0]
        for m in range(PIECE):
            recv[q][s * CAP + piece * PIECE + m] = rows[within(idx_s[wide, piece * PIECE + m], ROWS)]
        return carry

    lax.fori_loop(0, CAP // PIECE, pack_own, 0)

    for k in range(1, WIDE):
        metas[k].wait_recv()
    flag = None
    for k in range(WIDE):
        line = meta_r[k, GROUP:META, :].astype(F32)[0:8]
        pos_v[k] = line.astype(I32)
        flag = line if flag is None else jnp.maximum(flag, line)
    to_smem = pltpu.make_async_copy(pos_v, pos_s, local_sem.at[5])
    to_smem.start()
    flag_s[...] = flag
    flags = {s: remote(flag_s, flag_r.at[s], flag_ss.at[s], flag_rs.at[s], narrow_at(s // 2, s % 2))
             for s in range(1, NARROW)}
    for copy in flags.values():
        copy.start()

    for dy in DY_ORDER:
        for copy in weights[2 * dy]:
            copy.wait_recv()
        for copy in weights[2 * dy + 1]:
            copy.start()
    for copy in here[1:]:
        copy.wait()
    for s in (1, 3, 5, 7):
        for copy in weights[s]:
            copy.wait_recv()
    to_smem.wait()

    def spread(s, carry):
        lanes = lax.broadcasted_iota(I32, (REG * 4, 128), 1)
        line = lax.broadcasted_iota(I32, (REG * 4, 128), 0)
        channel = jnp.bitwise_and(line, 3)
        for j in range(REG):
            match = jnp.logical_and(jnp.right_shift(line, 2) == j, lanes == channel * GROUP + s * REG + j)
            wp[pl.ds((s * REG + j) * HID, HID)] = tn(wo[s], match.astype(BF16)).astype(BF16)
        return carry

    lax.fori_loop(0, NARROW, spread, 0)

    line = lax.broadcasted_iota(I32, (8 * SAMP, 8 * SAMP), 0)
    lane = lax.broadcasted_iota(I32, (8 * SAMP, 8 * SAMP), 1)
    same = jnp.zeros(line.shape, jnp.bool_)
    for b in range(8):
        inside = jnp.logical_and(line >= b * SAMP, line < (b + 1) * SAMP)
        same = jnp.logical_or(same, jnp.logical_and(inside, jnp.logical_and(lane >= b * SAMP, lane < (b + 1) * SAMP)))
    earlier = jnp.logical_and(same, line < lane).astype(F32)
    line = lax.broadcasted_iota(I32, (8, 8 * SAMP), 0)
    lane = lax.broadcasted_iota(I32, (8, 8 * SAMP), 1)
    pick = jnp.logical_and(lane >= line * SAMP, lane < (line + 1) * SAMP).astype(F32)

    returns = {}
    for q, chunk in enumerate(CHUNKS):
        for k in chunk:
            if k:
                data_copy(k, 0, CAP).wait_recv()
        acc[...] = jnp.zeros_like(acc)

        def regions(dy, carry, q=q, chunk=chunk):
            def rows_of(j):
                return jnp.concatenate(
                    [recv[q][s * CAP + within(pos_s[k, 0, ahead * GROUP + dy * 2 * REG + j], CAP)]
                     for s, k in enumerate(chunk) for ahead in range(2)], axis=0)

            span = range(2 * REG)
            hidden = [relu(dot(rows_of(j), wi[dy * 2 * REG + j])) for j in span]
            hidden = [relu(dot(hidden[j], wm[dy * 2 * REG + j, 0])) for j in span]
            hidden = [relu(dot(hidden[j], wm[dy * 2 * REG + j, 1])) for j in span]
            acc[...] += dot(jnp.concatenate(hidden, axis=1), wp[pl.ds(dy * 2 * REG * HID, 2 * REG * HID)])
            return carry

        lax.fori_loop(0, NARROW // 2, regions, 0)

        raw = acc[...].T
        gap = jnp.concatenate([meta_r[k, 0:GROUP, 0:2 * SAMP].astype(F32) for k in chunk], axis=1)
        density = raw[0:GROUP]
        density = jnp.maximum(density, 0.0) + jnp.log1p(jnp.exp(-jnp.abs(density)))
        optical = density * gap
        passed = jnp.exp(-dot(optical, earlier, lax.Precision.HIGHEST))
        series = optical * (1.0 - optical * (1 / 2 - optical * (1 / 6 - optical * (1 / 24 - optical * (1 / 120)))))
        weight = passed * jnp.where(optical < 0.125, series, 1.0 - jnp.exp(-optical))
        parts = [weight * jax.nn.sigmoid(raw[(c + 1) * GROUP:(c + 2) * GROUP]) for c in range(3)] + [optical]
        result = nt(pick, jnp.concatenate(parts, axis=0), lax.Precision.HIGHEST)
        for s, k in enumerate(chunk):
            target = ret_s if k else ret_r
            target[k, 0:2, :] = result[2 * s:2 * s + 2]
            if k:
                returns[k] = remote(ret_s.at[k], ret_r.at[k], ret_ss.at[k], ret_rs.at[k], wide_at(k, -1))
                returns[k].start()

    for k in range(1, WIDE):
        returns[k].wait_recv()
    back = jnp.concatenate([ret_r[k, 0:2, :] for k in range(WIDE)], axis=0)
    offset = jnp.bitwise_and(jnp.right_shift(g, 2) - z, 3) * 4 + jnp.bitwise_and(jnp.bitwise_and(g, 3) - x, 3)
    found = tn(back, onehot(2 * WIDE, offset * 2 + a_int).astype(F32), lax.Precision.HIGHEST)
    keep = onehot(GROUP, r).astype(F32)
    for c in range(4):
        fin_s[c:c + 1, :] = jnp.sum(found[c * GROUP:(c + 1) * GROUP] * keep, axis=0, keepdims=True)
    finals = {k: remote(fin_s, fin_r.at[wide], fin_ss.at[k], fin_rs.at[k], wide_at(k)) for k in range(1, WIDE)}
    for copy in finals.values():
        copy.start()
    fin_r[wide] = fin_s[...]
    for s in range(1, NARROW):
        flags[s].wait_recv()
        flag = jnp.maximum(flag, flag_r[s])
    for k in range(1, WIDE):
        remote(fin_s, fin_r.at[group_at(k, -1)], fin_ss.at[k], fin_rs.at[k], wide_at(k)).wait_recv()

    depth = [fin_r[s, 3:4, :] for s in range(WIDE)]
    ahead, behind = [jnp.zeros_like(depth[0])], [jnp.zeros_like(depth[0])]
    for s in range(WIDE - 1):
        ahead.append(ahead[-1] + depth[s])
        behind.append(behind[-1] + depth[WIDE - 1 - s])
    backward = dirs[...] == 1
    colour = jnp.zeros((3, ROWS), F32)
    for s in range(WIDE):
        light = jnp.exp(-jnp.where(backward, behind[WIDE - 1 - s], ahead[s]))
        colour = colour + light * fin_r[s, 0:3, :]
    out[0:3, :] = colour
    out[3:8, :] = jnp.broadcast_to(flag[0:1, FLAG:FLAG + 1], (5, ROWS))

    for s in range(1, NARROW):
        for copy in weights[s]:
            copy.wait_send()
        flags[s].wait_send()
    for k in range(1, WIDE):
        metas[k].wait_send()
        data_copy(k, 0, CAP).wait_send()
        returns[k].wait_send()
        finals[k].wait_send()


def render(samples, spacing, ids, dirs, w_in, w_mid, w_out):
    vmem, smem, dma = pltpu.VMEM, pltpu.SMEM, pltpu.SemaphoreType.DMA
    regions = NARROW * REG
    whole, any_place = pl.BlockSpec(memory_space=pltpu.VMEM), pl.BlockSpec(memory_space=pl.ANY)
    scratch = [vmem((ROWS, SAMP, FEAT), BF16), vmem((WIDE - 1, CAP, SAMP, FEAT), BF16)]
    scratch += [vmem((len(chunk) * CAP, SAMP, FEAT), BF16) for chunk in CHUNKS]
    scratch += [
        vmem((regions, FEAT, HID), BF16), vmem((regions, 2, HID, HID), BF16), vmem((NARROW, REG * 4, HID), BF16),
        vmem((regions * HID, 128), BF16), vmem((WIDE, META, 128), BF16), vmem((WIDE, META, 128), BF16),
        vmem((WIDE, 8, 128), I32), smem((WIDE, 8, 128), I32), vmem((WIDE, 128), I32), smem((WIDE, 128), I32),
        vmem((8 * SAMP, 128), F32), vmem((WIDE, 8, 128), F32), vmem((WIDE, 8, 128), F32),
        vmem((8, ROWS), F32), vmem((WIDE, 8, ROWS), F32), vmem((8, 128), F32), vmem((NARROW, 8, 128), F32),
        dma((6,)), dma((3, NARROW)), dma((3, NARROW)), dma((1,)), dma((WIDE,)), dma((WIDE,)), dma((WIDE,)),
        dma((WIDE,)), dma((WIDE,)), dma((WIDE,)), dma((WIDE,)), dma((WIDE,)), dma((NARROW,)), dma((NARROW,))]
    return pl.pallas_call(
        render_kernel,
        out_shape=jax.ShapeDtypeStruct((8, ROWS), F32),
        in_specs=[any_place, whole, whole, whole, any_place, any_place, any_place],
        out_specs=whole,
        scratch_shapes=scratch,
        compiler_params=pltpu.CompilerParams(collective_id=0, has_side_effects=True, vmem_limit_bytes=58 * 2**20),
        name="render",
    )(samples, spacing, ids, dirs, w_in, w_mid, w_out)


def on_device(samples, spacing, region_ids, directions, w_in, w_mid, w_out):
    args = (samples, spacing, region_ids, directions, w_in, w_mid, w_out)
    fast = render(
        samples.reshape(ROWS, SAMP, FEAT), spacing.reshape(ROWS, SAMP), region_ids.reshape(1, ROWS),
        directions.reshape(1, ROWS), w_in, w_mid, w_out.reshape(REG * 4, HID))
    return lax.cond(fast[3, 0] > 0, lambda rest: general(*rest), lambda rest: fast[0:3], args)


def solution(mesh):
    in_specs = (
        P("wide", "narrow", None, None),
        P("wide", "narrow", None),
        P("wide", "narrow", None),
        P("narrow"),
        P(("wide", "narrow"), None, None),
        P(("wide", "narrow"), None, None, None),
        P(("wide", "narrow"), None, None),
    )
    out_specs = P(None, "narrow")
    return jax.shard_map(
        on_device, mesh=mesh, in_specs=in_specs, out_specs=out_specs, check_vma=False
    )
```

```python
import jax
import jax.numpy as jnp
from jax import lax
from jax.experimental import pallas as pl
from jax.experimental.pallas import tpu as pltpu
from jax.sharding import PartitionSpec as P

MESH = pl.DeviceIdType.MESH
F32, BF16, I32 = jnp.float32, jnp.bfloat16, jnp.int32
ROWS, SAMP, FEAT, HID = 512, 48, 128, 256
WIDE, NARROW, REG, GROUP = 16, 8, 4, 32
CAP = 40
PIECE = 8
META = 48
FLAG = 127

SEND_ORDER = ((6, 14, 9, 11, 1, 3, 4, 12), (2, 8, 10))
HELD = {0: ((5, 15),), 1: ((7, 13),)}
CHUNKS = ((0, 6, 14, 9), (11, 1, 3, 4), (12, 2, 8, 10), (5, 15), (7, 13))
MOST = 4 * 2 * SAMP


def nt(a, b):
    return lax.dot_general(a, b, (((1,), (1,)), ((), ())), preferred_element_type=F32)


def tn(a, b):
    return lax.dot_general(a, b, (((0,), (0,)), ((), ())), preferred_element_type=F32)


def dot(a, b):
    return jnp.dot(a, b, preferred_element_type=F32)


def halves(v):
    high = v.astype(BF16)
    return jnp.concatenate([high, (v - high.astype(F32)).astype(BF16)], axis=0)


def onehot(rows, lanes_value):
    return lax.broadcasted_iota(I32, (rows, lanes_value.shape[1]), 0) == lanes_value


def within(i, size):
    return jnp.minimum(jnp.maximum(i, 0), size - 1)


def relu(v):
    return jnp.maximum(v.astype(BF16), 0)


def prefix_2(array, axis, combine, identity, reverse):
    count, position = (lax.axis_size(axis), lax.axis_index(axis))
    everything = lax.all_gather(array, axis)
    start = jnp.broadcast_to(jnp.asarray(identity, array.dtype), array.shape)

    def hop(k, before):
        at = count - 1 - k if reverse else k
        reached = at > position if reverse else at < position
        new = combine(before, everything[at])
        return jnp.where(reached, new, before)

    return lax.fori_loop(0, count, hop, start)


def composite(raw_out, spacing_part):
    density = jax.nn.softplus(raw_out[0])
    colours = jax.nn.sigmoid(raw_out[1:4])
    optical = density * spacing_part.astype(jnp.float32)
    before_sum = jnp.cumsum(optical, axis=-1) - optical
    sample_weight = jnp.exp(-before_sum) * -jnp.expm1(-optical)
    seg_colour = jnp.sum(sample_weight * colours, axis=-1)
    seg_depth = jnp.sum(optical, axis=-1)
    return jnp.stack([seg_colour[0], seg_colour[1], seg_colour[2], seg_depth], axis=-1)


def accumulate(earlier, later):
    return earlier + later


def general(samples, spacing, region_ids, directions, w_in, w_mid, w_out):
    wide_size = lax.axis_size("wide")
    narrow_size = lax.axis_size("narrow")
    devices_all = wide_size * narrow_size
    reg_local = w_in.shape[0]
    ray_local = samples.shape[1]
    sample_len = samples.shape[2]
    width_in = samples.shape[3]
    region_all = reg_local * devices_all
    capacity = max(2, 2 * ray_local // region_all)
    slot_total = region_all * capacity
    region_row = region_ids.reshape(ray_local)
    matches = region_row[:, None] == region_row[None, :]
    positions = jnp.arange(ray_local, dtype=jnp.int32)
    earlier = positions[None, :] < positions[:, None]
    arrival = jnp.sum(jnp.logical_and(matches, earlier), axis=1)
    slot_index = region_row * capacity + arrival
    source_row = jnp.full((slot_total,), ray_local, jnp.int32).at[slot_index].set(positions)
    ray_rows = jnp.concatenate(
        [
            samples.reshape(ray_local, sample_len, width_in),
            jnp.zeros((1, sample_len, width_in), samples.dtype),
        ],
        axis=0,
    )
    gap_rows = jnp.concatenate(
        [spacing.reshape(ray_local, sample_len), jnp.zeros((1, sample_len), spacing.dtype)], axis=0
    )
    send_features = jnp.take(ray_rows, source_row, axis=0)
    send_spacing = jnp.take(gap_rows, source_row, axis=0)
    features = lax.all_to_all(
        send_features.reshape(devices_all, reg_local, capacity, sample_len, width_in),
        ("wide", "narrow"),
        split_axis=0,
        concat_axis=0,
        tiled=True,
    )
    spacing_part = lax.all_to_all(
        send_spacing.reshape(devices_all, reg_local, capacity, sample_len),
        ("wide", "narrow"),
        split_axis=0,
        concat_axis=0,
        tiled=True,
    )
    results = []
    for region in range(reg_local):
        inputs = features[:, region].reshape(-1, width_in)
        hidden = jax.nn.relu(
            jnp.dot(inputs, w_in[region], preferred_element_type=jnp.float32)
        ).astype(jnp.bfloat16)
        for layer_index in range(w_mid.shape[1]):
            hidden = jax.nn.relu(
                jnp.dot(hidden, w_mid[region, layer_index], preferred_element_type=jnp.float32)
            ).astype(jnp.bfloat16)
        raw_out = jnp.einsum("nh,ch->cn", hidden, w_out[region], preferred_element_type=jnp.float32)
        part_gap = spacing_part[:, region]
        raw_out = raw_out.reshape((4,) + part_gap.shape)
        results.append(composite(raw_out, part_gap))
    partial_here = jnp.stack(results, axis=1)
    returned = lax.all_to_all(
        partial_here, ("wide", "narrow"), split_axis=0, concat_axis=0, tiled=True
    )
    mine = jnp.take(returned.reshape(slot_total, 4), slot_index, axis=0)
    seg_depth = mine[:, 3]
    zero_depth = jnp.zeros_like(seg_depth)
    ahead = prefix_2(seg_depth, "wide", accumulate, zero_depth, False)
    behind = prefix_2(seg_depth, "wide", accumulate, zero_depth, True)
    prefix = jnp.where(directions == 1, behind, ahead)
    light = jnp.exp(-prefix)
    light_term = (light[:, None] * mine[:, :3]).T
    return lax.psum(light_term, "wide")


def render_kernel(samples, spacing, ids, dirs, w_in, w_mid, w_out, out, over_out, *scratch):
    (rows, send, recv0, recv1, recv2, recv3, recv4, wi, wm, wo, wp, meta_s, meta_r, pos_v, pos_s, idx_v, idx_s, acc,
     earlier, pick, where_row, keep, ret_s, ret_r, fin_s, fin_r, flag_s, flag_r, local_sem, wt_send, wt_recv,
     meta_ss, meta_rs, data_ss, data_rs, ret_ss, ret_rs, fin_ss, fin_rs, flag_ss, flag_rs) = scratch
    recv = (recv0, recv1, recv2, recv3, recv4)
    place = {k: (q, s) for q, chunk in enumerate(CHUNKS) for s, k in enumerate(chunk)}
    wide, nar = lax.axis_index("wide"), lax.axis_index("narrow")
    z, x = wide // 4, wide % 4
    y, core = nar // 2, nar % 2

    def group_at(k, sign=1):
        return ((z + sign * (k // 4) + 4) % 4) * 4 + (x + sign * (k % 4) + 4) % 4

    def wide_at(k, sign=1):
        return (group_at(k, sign), nar)

    def narrow_at(dy, dc):
        return (wide, ((y + dy + 4) % 4) * 2 + (core + dc) % 2)

    def remote(src, dst, ss, rs, to):
        return pltpu.make_async_remote_copy(
            src_ref=src, dst_ref=dst, send_sem=ss, recv_sem=rs, device_id=to, device_id_type=MESH)

    barrier = pltpu.get_barrier_semaphore()
    for k in range(1, WIDE):
        pl.semaphore_signal(barrier, inc=1, device_id=wide_at(k), device_id_type=MESH)
    for t in range(1, NARROW):
        pl.semaphore_signal(barrier, inc=1, device_id=narrow_at(t // 2, t % 2), device_id_type=MESH)

    quarter = ROWS // 4
    own_rows = [pltpu.make_async_copy(samples.at[pl.ds(i * quarter, quarter)], rows.at[pl.ds(i * quarter, quarter)],
                                      local_sem.at[i]) for i in range(4)]
    own_weights = [pltpu.make_async_copy(w_in, wi.at[pl.ds(0, REG)], local_sem.at[4]),
                   pltpu.make_async_copy(w_mid, wm.at[pl.ds(0, REG)], local_sem.at[5]),
                   pltpu.make_async_copy(w_out, wo.at[0], local_sem.at[6])]
    for copy in own_rows + own_weights:
        copy.start()

    rid = ids[...]
    g = jnp.right_shift(rid, 5)
    ray = lax.broadcasted_iota(I32, (1, ROWS), 1)
    before = (lax.broadcasted_iota(I32, (ROWS, ROWS), 0) < lax.broadcasted_iota(I32, (ROWS, ROWS), 1)).astype(BF16)
    of_group = onehot(WIDE, g).astype(F32)
    p = jnp.sum(of_group * dot(of_group.astype(BF16), before), axis=0, keepdims=True)
    at_place = onehot(128, p.astype(I32)).astype(BF16)
    low = of_group * jnp.bitwise_and(ray, 15).astype(F32)
    high = of_group * jnp.right_shift(ray, 4).astype(F32)
    source = nt(jnp.concatenate([low, high], axis=0).astype(BF16), at_place)
    idx_v[...] = (source[0:WIDE] + 16.0 * source[WIDE:2 * WIDE]).astype(I32)
    to_smem = pltpu.make_async_copy(idx_v, idx_s, local_sem.at[7])
    to_smem.start()

    pl.semaphore_wait(barrier, WIDE - 1 + NARROW - 1)

    half = REG // 2

    def weight_copies(s, to, taken_from=None):
        copies = []
        for h in range(2):
            for ref, own in ((wi, w_in), (wm, w_mid)):
                src = own.at[pl.ds(h * half, half)] if taken_from is None else ref.at[pl.ds(taken_from * REG + h * half, half)]
                i = 2 * h + (0 if ref is wi else 1)
                copies.append(remote(src, ref.at[pl.ds(s * REG + h * half, half)], wt_send.at[i, s], wt_recv.at[i, s], to))
        src = w_out if taken_from is None else wo.at[taken_from]
        return copies + [remote(src, wo.at[s], wt_send.at[4, s], wt_recv.at[4, s], to)]

    weights = {1: weight_copies(1, narrow_at(0, 1)), 2: weight_copies(2, narrow_at(-1, 0)),
               6: weight_copies(6, narrow_at(1, 0)), 3: weight_copies(3, narrow_at(0, 1), 2),
               7: weight_copies(7, narrow_at(0, 1), 6), 5: weight_copies(5, narrow_at(0, 1), 4)}
    weights[4] = weight_copies(4, narrow_at(-1, 0), 2)[0:2] + weight_copies(4, narrow_at(1, 0), 6)[2:4]
    weights[4] += weight_copies(4, narrow_at(2, 0))[4:5]
    first, second, last = slice(0, 2), slice(2, 4), slice(4, 5)

    def start(s, part):
        for copy in weights[s][part]:
            copy.start()

    def arrived(s, part):
        for copy in weights[s][part]:
            copy.wait_recv()

    for s, part in ((2, last), (6, last), (4, last), (2, first), (6, second), (2, second), (6, first),
                    (1, last), (1, first), (1, second)):
        start(s, part)

    for copy in own_rows:
        copy.wait()
    to_smem.wait()

    def data_copy(k, begin, size):
        q, s = place[k]
        return remote(send.at[k - 1, pl.ds(begin, size)], recv[q].at[pl.ds(s * CAP + begin, size)],
                      data_ss.at[k], data_rs.at[k], wide_at(k))

    def pack(piece, order):
        for k in order:
            to = group_at(k)
            for m in range(PIECE):
                send[k - 1, piece * PIECE + m] = rows[within(idx_s[to, piece * PIECE + m], ROWS)]
            data_copy(k, piece * PIECE, PIECE).start()

    pack(0, SEND_ORDER[0])

    nb = jnp.bitwise_and(jnp.right_shift(rid, 2), 7)
    t = jnp.bitwise_and(jnp.right_shift(nb, 1) - y, 3) * 2 + jnp.bitwise_and(nb + core, 1)
    r = t * REG + jnp.bitwise_and(rid, 3)
    of_region = onehot(WIDE * GROUP, g * GROUP + r).astype(BF16)
    a = jnp.sum(of_region.astype(F32) * dot(of_region, before), axis=0, keepdims=True)
    a_int = a.astype(I32)
    slot = onehot(128, a_int * GROUP + r).astype(BF16)
    position = nt((of_group * jnp.minimum(p, CAP - 1.0)).astype(BF16), slot)
    over = (jnp.max(p, axis=1, keepdims=True) >= CAP).astype(F32)
    position = jnp.where(lax.broadcasted_iota(I32, (WIDE, 128), 1) == FLAG, over, position)
    gaps = spacing[...].astype(F32)
    gaps = jnp.concatenate([gaps * (1.0 - a), gaps * a, jnp.zeros((128 - 2 * SAMP, ROWS), F32)], axis=0).astype(BF16)
    meta_s[:, 0:GROUP, :] = nt(of_region, gaps).astype(BF16).reshape(WIDE, GROUP, 128)
    for w in range(WIDE):
        meta_s[w, GROUP:META, :] = jnp.broadcast_to(position[w:w + 1], (META - GROUP, 128)).astype(BF16)
    meta_r[0] = meta_s[wide]
    metas = {k: remote(meta_s.at[group_at(k)], meta_r.at[k], meta_ss.at[k], meta_rs.at[k], wide_at(k))
             for k in range(1, WIDE)}
    for copy in metas.values():
        copy.start()

    def pack_all(order, begin=0):
        def step(piece, carry):
            pack(piece, order)
            return carry

        lax.fori_loop(begin, CAP // PIECE, step, 0)

    for i, order in enumerate(SEND_ORDER):
        pack_all(order, 1 if i == 0 else 0)

    def pack_own(piece, carry):
        q, s = place[0]
        for m in range(PIECE):
            recv[q][s * CAP + piece * PIECE + m] = rows[within(idx_s[wide, piece * PIECE + m], ROWS)]
        return carry

    lax.fori_loop(0, CAP // PIECE, pack_own, 0)

    offset = jnp.bitwise_and(jnp.right_shift(g, 2) - z, 3) * 4 + jnp.bitwise_and(jnp.bitwise_and(g, 3) - x, 3)
    came = onehot(2 * WIDE, offset * 2 + a_int).astype(F32)
    where_row[...] = jnp.concatenate([came, came], axis=0).astype(BF16)
    keep[...] = onehot(GROUP, r).astype(F32)
    line = lax.broadcasted_iota(I32, (MOST, MOST), 0)
    lane = lax.broadcasted_iota(I32, (MOST, MOST), 1)
    same = jnp.zeros((MOST, MOST), jnp.bool_)
    for b in range(MOST // SAMP):
        ends = (b * SAMP, (b + 1) * SAMP)
        same = jnp.logical_or(same, jnp.logical_and(jnp.logical_and(line >= ends[0], line < ends[1]),
                                                    jnp.logical_and(lane >= ends[0], lane < ends[1])))
    earlier[...] = jnp.logical_and(same, line < lane).astype(BF16)
    line = lax.broadcasted_iota(I32, (16, MOST), 0)
    lane = lax.broadcasted_iota(I32, (16, MOST), 1)
    pick[...] = jnp.logical_and(lane >= line * SAMP, lane < (line + 1) * SAMP).astype(BF16)

    for k in range(1, WIDE):
        metas[k].wait_recv()
    flag = None
    for k in range(WIDE):
        line = meta_r[k, GROUP:META, :].astype(F32)[0:8]
        pos_v[k] = line.astype(I32)
        flag = line if flag is None else jnp.maximum(flag, line)
    to_smem = pltpu.make_async_copy(pos_v, pos_s, local_sem.at[8])
    to_smem.start()
    flag_s[...] = flag
    flags = {s: remote(flag_s, flag_r.at[s], flag_ss.at[s], flag_rs.at[s], narrow_at(s // 2, s % 2))
             for s in range(1, NARROW)}
    for copy in flags.values():
        copy.start()

    for s in (2, 6, 4):
        arrived(s, last)
        start(s + 1, last)
    own_weights[2].wait()
    for s in (1, 3, 7, 5):
        arrived(s, last)

    def spread(s, carry):
        lanes = lax.broadcasted_iota(I32, (REG * 4, 128), 1)
        line = lax.broadcasted_iota(I32, (REG * 4, 128), 0)
        channel = jnp.bitwise_and(line, 3)
        heads = wo[s].astype(F32).reshape(REG * 4, HID).astype(BF16)
        for j in range(REG):
            match = jnp.logical_and(jnp.right_shift(line, 2) == j, lanes == channel * GROUP + s * REG + j)
            wp[pl.ds((s * REG + j) * HID, HID)] = tn(heads, match.astype(BF16)).astype(BF16)
        return carry

    lax.fori_loop(0, NARROW, spread, 0)

    arrived(2, first), start(4, first), start(3, first)
    arrived(6, second), start(4, second), start(7, second)
    arrived(2, second), start(3, second)
    arrived(6, first), start(7, first)
    own_weights[0].wait(), own_weights[1].wait()
    for s in (1, 3, 7):
        arrived(s, first), arrived(s, second)
    arrived(4, first), start(5, first)
    arrived(4, second), start(5, second)
    arrived(5, first), arrived(5, second)
    to_smem.wait()

    returns = {}
    for q, chunk in enumerate(CHUNKS):
        size = len(chunk) * 2 * SAMP
        for k in chunk:
            if k:
                data_copy(k, 0, CAP).wait_recv()
        for order in HELD.get(q, ()):
            pack_all(order)
        acc[...] = jnp.zeros_like(acc)

        def regions(dy, carry, q=q, chunk=chunk, size=size):
            def rows_of(j):
                return jnp.concatenate(
                    [recv[q][s * CAP + within(pos_s[k, 0, ahead * GROUP + dy * 2 * REG + j], CAP)]
                     for s, k in enumerate(chunk) for ahead in range(2)], axis=0)

            span = range(2 * REG)
            hidden = [relu(dot(rows_of(j), wi[dy * 2 * REG + j])) for j in span]
            hidden = [relu(dot(hidden[j], wm[dy * 2 * REG + j, 0])) for j in span]
            hidden = [relu(dot(hidden[j], wm[dy * 2 * REG + j, 1])) for j in span]
            acc[0:size] += dot(jnp.concatenate(hidden, axis=1), wp[pl.ds(dy * 2 * REG * HID, 2 * REG * HID)])
            return carry

        lax.fori_loop(0, NARROW // 2, regions, 0)

        raw = acc[0:size].T
        gap = jnp.concatenate([meta_r[k, 0:GROUP, 0:2 * SAMP].astype(F32) for k in chunk], axis=1)
        density = raw[0:GROUP]
        density = jnp.maximum(density, 0.0) + jnp.log1p(jnp.exp(-jnp.abs(density)))
        optical = density * gap
        sums = dot(halves(optical), earlier[0:size, 0:size])
        passed = jnp.exp(-(sums[0:GROUP] + sums[GROUP:2 * GROUP]))
        series = optical * (1.0 - optical * (1 / 2 - optical * (1 / 6 - optical * (1 / 24 - optical * (1 / 120)))))
        weight = passed * jnp.where(optical < 0.125, series, 1.0 - jnp.exp(-optical))
        parts = [weight * jax.nn.sigmoid(raw[(c + 1) * GROUP:(c + 2) * GROUP]) for c in range(3)] + [optical]
        result = nt(pick[:, 0:size], halves(jnp.concatenate(parts, axis=0)))
        result = result[:, 0:128] + result[:, 128:256]
        for s, k in enumerate(chunk):
            target = ret_s if k else ret_r
            target[k, 0:2, :] = result[2 * s:2 * s + 2]
            if k:
                returns[k] = remote(ret_s.at[k], ret_r.at[k], ret_ss.at[k], ret_rs.at[k], wide_at(k, -1))
                returns[k].start()

    for k in range(1, WIDE):
        returns[k].wait_recv()
    back = jnp.concatenate([ret_r[k, 0:2, :] for k in range(WIDE)], axis=0)
    found = tn(halves(back), where_row[...])
    for c in range(4):
        fin_s[c:c + 1, :] = jnp.sum(found[c * GROUP:(c + 1) * GROUP] * keep[...], axis=0, keepdims=True)
    finals = {k: remote(fin_s, fin_r.at[wide], fin_ss.at[k], fin_rs.at[k], wide_at(k)) for k in range(1, WIDE)}
    for copy in finals.values():
        copy.start()
    fin_r[wide] = fin_s[...]
    for s in range(1, NARROW):
        flags[s].wait_recv()
        flag = jnp.maximum(flag, flag_r[s])
    over_out[...] = jnp.broadcast_to(flag[0:1, FLAG:FLAG + 1], (1, 128))
    for s in range(1, NARROW):
        for copy in weights[s]:
            copy.wait_send()
        flags[s].wait_send()
    for k in range(1, WIDE):
        metas[k].wait_send()
        data_copy(k, 0, CAP).wait_send()
        returns[k].wait_send()
    for k in range(1, WIDE):
        remote(fin_s, fin_r.at[group_at(k, -1)], fin_ss.at[k], fin_rs.at[k], wide_at(k)).wait_recv()

    depth = [fin_r[s, 3:4, :] for s in range(WIDE)]
    ahead, behind = [jnp.zeros_like(depth[0])], [jnp.zeros_like(depth[0])]
    for s in range(WIDE - 1):
        ahead.append(ahead[-1] + depth[s])
        behind.append(behind[-1] + depth[WIDE - 1 - s])
    backward = dirs[...] == 1
    colour = jnp.zeros((3, ROWS), F32)
    for s in range(WIDE):
        light = jnp.exp(-jnp.where(backward, behind[WIDE - 1 - s], ahead[s]))
        colour = colour + light * fin_r[s, 0:3, :]
    out[...] = colour
    for k in range(1, WIDE):
        finals[k].wait_send()


def render(samples, spacing, ids, dirs, w_in, w_mid, w_out):
    vmem, smem, dma = pltpu.VMEM, pltpu.SMEM, pltpu.SemaphoreType.DMA
    regions = NARROW * REG
    whole, any_place = pl.BlockSpec(memory_space=pltpu.VMEM), pl.BlockSpec(memory_space=pl.ANY)
    scratch = [vmem((ROWS, SAMP, FEAT), BF16), vmem((WIDE - 1, CAP, SAMP, FEAT), BF16)]
    scratch += [vmem((len(chunk) * CAP, SAMP, FEAT), BF16) for chunk in CHUNKS]
    scratch += [
        vmem((regions, FEAT, HID), BF16), vmem((regions, 2, HID, HID), BF16), vmem((NARROW, REG, 4, HID), BF16),
        vmem((regions * HID, 128), BF16), vmem((WIDE, META, 128), BF16), vmem((WIDE, META, 128), BF16),
        vmem((WIDE, 8, 128), I32), smem((WIDE, 8, 128), I32), vmem((WIDE, 128), I32), smem((WIDE, 128), I32),
        vmem((MOST, 128), F32), vmem((MOST, MOST), BF16), vmem((16, MOST), BF16), vmem((4 * WIDE, ROWS), BF16),
        vmem((GROUP, ROWS), F32), vmem((WIDE, 8, 128), F32), vmem((WIDE, 8, 128), F32),
        vmem((8, ROWS), F32), vmem((WIDE, 8, ROWS), F32), vmem((8, 128), F32), vmem((NARROW, 8, 128), F32),
        dma((9,)), dma((5, NARROW)), dma((5, NARROW)), dma((WIDE,)), dma((WIDE,)), dma((WIDE,)),
        dma((WIDE,)), dma((WIDE,)), dma((WIDE,)), dma((WIDE,)), dma((WIDE,)), dma((NARROW,)), dma((NARROW,))]
    return pl.pallas_call(
        render_kernel,
        out_shape=(jax.ShapeDtypeStruct((3, ROWS), F32), jax.ShapeDtypeStruct((1, 128), F32)),
        in_specs=[any_place, whole, whole, whole, any_place, any_place, any_place],
        out_specs=(whole, whole),
        scratch_shapes=scratch,
        compiler_params=pltpu.CompilerParams(collective_id=0, has_side_effects=True, vmem_limit_bytes=58 * 2**20),
        name="render",
    )(samples, spacing, ids, dirs, w_in, w_mid, w_out)


def on_device(samples, spacing, region_ids, directions, w_in, w_mid, w_out):
    args = (samples, spacing, region_ids, directions, w_in, w_mid, w_out)
    fast, over = render(
        samples.reshape(ROWS, SAMP, FEAT), spacing.reshape(ROWS, SAMP).T, region_ids.reshape(1, ROWS),
        directions.reshape(1, ROWS), w_in, w_mid, w_out)
    return lax.cond(over[0, 0] > 0, lambda rest: general(*rest), lambda rest: fast, args)


def solution(mesh):
    in_specs = (
        P("wide", "narrow", None, None),
        P("wide", "narrow", None),
        P("wide", "narrow", None),
        P("narrow"),
        P(("wide", "narrow"), None, None),
        P(("wide", "narrow"), None, None, None),
        P(("wide", "narrow"), None, None),
    )
    out_specs = P(None, "narrow")
    return jax.shard_map(
        on_device, mesh=mesh, in_specs=in_specs, out_specs=out_specs, check_vma=False
    )
```

```python
import jax
import jax.numpy as jnp
from jax import lax
from jax.experimental import pallas as pl
from jax.experimental.pallas import tpu as pltpu
from jax.sharding import PartitionSpec as P

MESH = pl.DeviceIdType.MESH
F32, BF16, I32 = jnp.float32, jnp.bfloat16, jnp.int32
ROWS, SAMP, FEAT, HID = 512, 48, 128, 256
WIDE, NARROW, REG, GROUP = 16, 8, 4, 32
CAP = 40
PIECE = 8
FLAG = 127

SEND_ORDER = ((6, 14, 9, 11, 1, 3, 4, 12), (2, 8, 10))
HELD = {0: ((5, 15),), 1: ((7, 13),)}
CHUNKS = ((0, 6, 14, 9), (11, 1, 3, 4), (12, 2, 8, 10), (5, 15), (7, 13))
MOST = 4 * 2 * SAMP


def nt(a, b):
    return lax.dot_general(a, b, (((1,), (1,)), ((), ())), preferred_element_type=F32)


def tn(a, b):
    return lax.dot_general(a, b, (((0,), (0,)), ((), ())), preferred_element_type=F32)


def dot(a, b):
    return jnp.dot(a, b, preferred_element_type=F32)


def halves(v):
    high = v.astype(BF16)
    return jnp.concatenate([high, (v - high.astype(F32)).astype(BF16)], axis=0)


def onehot(rows, lanes_value):
    return lax.broadcasted_iota(I32, (rows, lanes_value.shape[1]), 0) == lanes_value


def within(i, size):
    return jnp.minimum(jnp.maximum(i, 0), size - 1)


def relu(v):
    return jnp.maximum(v.astype(BF16), 0)


def prefix_2(array, axis, combine, identity, reverse):
    count, position = (lax.axis_size(axis), lax.axis_index(axis))
    everything = lax.all_gather(array, axis)
    start = jnp.broadcast_to(jnp.asarray(identity, array.dtype), array.shape)

    def hop(k, before):
        at = count - 1 - k if reverse else k
        reached = at > position if reverse else at < position
        new = combine(before, everything[at])
        return jnp.where(reached, new, before)

    return lax.fori_loop(0, count, hop, start)


def composite(raw_out, spacing_part):
    density = jax.nn.softplus(raw_out[0])
    colours = jax.nn.sigmoid(raw_out[1:4])
    optical = density * spacing_part.astype(jnp.float32)
    before_sum = jnp.cumsum(optical, axis=-1) - optical
    sample_weight = jnp.exp(-before_sum) * -jnp.expm1(-optical)
    seg_colour = jnp.sum(sample_weight * colours, axis=-1)
    seg_depth = jnp.sum(optical, axis=-1)
    return jnp.stack([seg_colour[0], seg_colour[1], seg_colour[2], seg_depth], axis=-1)


def accumulate(earlier, later):
    return earlier + later


def general(samples, spacing, region_ids, directions, w_in, w_mid, w_out):
    wide_size = lax.axis_size("wide")
    narrow_size = lax.axis_size("narrow")
    devices_all = wide_size * narrow_size
    reg_local = w_in.shape[0]
    ray_local = samples.shape[1]
    sample_len = samples.shape[2]
    width_in = samples.shape[3]
    region_all = reg_local * devices_all
    capacity = max(2, 2 * ray_local // region_all)
    slot_total = region_all * capacity
    region_row = region_ids.reshape(ray_local)
    matches = region_row[:, None] == region_row[None, :]
    positions = jnp.arange(ray_local, dtype=jnp.int32)
    earlier = positions[None, :] < positions[:, None]
    arrival = jnp.sum(jnp.logical_and(matches, earlier), axis=1)
    slot_index = region_row * capacity + arrival
    source_row = jnp.full((slot_total,), ray_local, jnp.int32).at[slot_index].set(positions)
    ray_rows = jnp.concatenate(
        [
            samples.reshape(ray_local, sample_len, width_in),
            jnp.zeros((1, sample_len, width_in), samples.dtype),
        ],
        axis=0,
    )
    gap_rows = jnp.concatenate(
        [spacing.reshape(ray_local, sample_len), jnp.zeros((1, sample_len), spacing.dtype)], axis=0
    )
    send_features = jnp.take(ray_rows, source_row, axis=0)
    send_spacing = jnp.take(gap_rows, source_row, axis=0)
    features = lax.all_to_all(
        send_features.reshape(devices_all, reg_local, capacity, sample_len, width_in),
        ("wide", "narrow"),
        split_axis=0,
        concat_axis=0,
        tiled=True,
    )
    spacing_part = lax.all_to_all(
        send_spacing.reshape(devices_all, reg_local, capacity, sample_len),
        ("wide", "narrow"),
        split_axis=0,
        concat_axis=0,
        tiled=True,
    )
    results = []
    for region in range(reg_local):
        inputs = features[:, region].reshape(-1, width_in)
        hidden = jax.nn.relu(
            jnp.dot(inputs, w_in[region], preferred_element_type=jnp.float32)
        ).astype(jnp.bfloat16)
        for layer_index in range(w_mid.shape[1]):
            hidden = jax.nn.relu(
                jnp.dot(hidden, w_mid[region, layer_index], preferred_element_type=jnp.float32)
            ).astype(jnp.bfloat16)
        raw_out = jnp.einsum("nh,ch->cn", hidden, w_out[region], preferred_element_type=jnp.float32)
        part_gap = spacing_part[:, region]
        raw_out = raw_out.reshape((4,) + part_gap.shape)
        results.append(composite(raw_out, part_gap))
    partial_here = jnp.stack(results, axis=1)
    returned = lax.all_to_all(
        partial_here, ("wide", "narrow"), split_axis=0, concat_axis=0, tiled=True
    )
    mine = jnp.take(returned.reshape(slot_total, 4), slot_index, axis=0)
    seg_depth = mine[:, 3]
    zero_depth = jnp.zeros_like(seg_depth)
    ahead = prefix_2(seg_depth, "wide", accumulate, zero_depth, False)
    behind = prefix_2(seg_depth, "wide", accumulate, zero_depth, True)
    prefix = jnp.where(directions == 1, behind, ahead)
    light = jnp.exp(-prefix)
    light_term = (light[:, None] * mine[:, :3]).T
    return lax.psum(light_term, "wide")


def render_kernel(samples, spacing, ids, dirs, w_in, w_mid, w_out, out, over_out, *scratch):
    rows, send, *recv = scratch[0:2 + len(CHUNKS)]
    (wi, wm, wo, wp, meta_s, meta_r, pos_t, pos_v, pos_s, idx_v, idx_s, acc,
     earlier, pick, where_row, keep, ret_s, ret_r, fin_s, fin_r, flag_s, flag_r, local_sem, wt_send, wt_recv,
     meta_ss, meta_rs, pos_ss, pos_rs, data_ss, data_rs, ret_ss, ret_rs, fin_ss, fin_rs, flag_ss, flag_rs) = scratch[2 + len(CHUNKS):]
    place = {k: (q, s) for q, chunk in enumerate(CHUNKS) for s, k in enumerate(chunk)}
    wide, nar = lax.axis_index("wide"), lax.axis_index("narrow")
    z, x = wide // 4, wide % 4
    y, core = nar // 2, nar % 2

    way = 1 - 2 * core

    def group_at(k, sign=1):
        return ((z + sign * way * (k // 4) + 4) % 4) * 4 + (x + sign * way * (k % 4) + 4) % 4

    def wide_at(k, sign=1):
        return (group_at(k, sign), nar)

    def narrow_at(dy, dc):
        return (wide, ((y + dy + 4) % 4) * 2 + (core + dc) % 2)

    def remote(src, dst, ss, rs, to):
        return pltpu.make_async_remote_copy(
            src_ref=src, dst_ref=dst, send_sem=ss, recv_sem=rs, device_id=to, device_id_type=MESH)

    barrier = pltpu.get_barrier_semaphore()
    for k in range(1, WIDE):
        pl.semaphore_signal(barrier, inc=1, device_id=wide_at(k), device_id_type=MESH)
    for t in range(1, NARROW):
        pl.semaphore_signal(barrier, inc=1, device_id=narrow_at(t // 2, t % 2), device_id_type=MESH)

    quarter = ROWS // 4
    own_rows = [pltpu.make_async_copy(samples.at[pl.ds(i * quarter, quarter)], rows.at[pl.ds(i * quarter, quarter)],
                                      local_sem.at[i]) for i in range(4)]
    own_weights = [pltpu.make_async_copy(w_in, wi.at[pl.ds(0, REG)], local_sem.at[4]),
                   pltpu.make_async_copy(w_mid, wm.at[pl.ds(0, REG)], local_sem.at[5]),
                   pltpu.make_async_copy(w_out, wo.at[0], local_sem.at[6])]
    for copy in own_rows + own_weights:
        copy.start()

    rid = ids[...]
    g = jnp.right_shift(rid, 5)
    ray = lax.broadcasted_iota(I32, (1, ROWS), 1)
    before = (lax.broadcasted_iota(I32, (ROWS, ROWS), 0) < lax.broadcasted_iota(I32, (ROWS, ROWS), 1)).astype(BF16)
    of_group = onehot(WIDE, g).astype(F32)
    p = jnp.sum(of_group * dot(of_group.astype(BF16), before), axis=0, keepdims=True)
    at_place = onehot(128, p.astype(I32)).astype(BF16)
    low = of_group * jnp.bitwise_and(ray, 15).astype(F32)
    high = of_group * jnp.right_shift(ray, 4).astype(F32)
    source = nt(jnp.concatenate([low, high], axis=0).astype(BF16), at_place)
    idx_v[...] = (source[0:WIDE] + 16.0 * source[WIDE:2 * WIDE]).astype(I32)
    to_smem = pltpu.make_async_copy(idx_v, idx_s, local_sem.at[7])
    to_smem.start()

    pl.semaphore_wait(barrier, WIDE - 1 + NARROW - 1)

    half = REG // 2

    def weight_copies(s, to, taken_from=None):
        copies = []
        for h in range(2):
            for ref, own in ((wi, w_in), (wm, w_mid)):
                src = own.at[pl.ds(h * half, half)] if taken_from is None else ref.at[pl.ds(taken_from * REG + h * half, half)]
                i = 2 * h + (0 if ref is wi else 1)
                copies.append(remote(src, ref.at[pl.ds(s * REG + h * half, half)], wt_send.at[i, s], wt_recv.at[i, s], to))
        src = w_out if taken_from is None else wo.at[taken_from]
        return copies + [remote(src, wo.at[s], wt_send.at[4, s], wt_recv.at[4, s], to)]

    weights = {1: weight_copies(1, narrow_at(0, 1)), 2: weight_copies(2, narrow_at(-1, 0)),
               6: weight_copies(6, narrow_at(1, 0)), 3: weight_copies(3, narrow_at(0, 1), 2),
               7: weight_copies(7, narrow_at(0, 1), 6), 5: weight_copies(5, narrow_at(0, 1), 4)}
    weights[4] = weight_copies(4, narrow_at(-1, 0), 2)[0:2] + weight_copies(4, narrow_at(1, 0), 6)[2:4]
    weights[4] += weight_copies(4, narrow_at(2, 0))[4:5]
    first, second, last = slice(0, 2), slice(2, 4), slice(4, 5)

    def start(s, part):
        for copy in weights[s][part]:
            copy.start()

    def arrived(s, part):
        for copy in weights[s][part]:
            copy.wait_recv()

    for copy in own_rows:
        copy.wait()
    to_smem.wait()

    def data_copy(k, begin, size):
        q, s = place[k]
        return remote(send.at[k - 1, pl.ds(begin, size)], recv[q].at[pl.ds(s * CAP + begin, size)],
                      data_ss.at[k], data_rs.at[k], wide_at(k))

    def pack(piece, order):
        for k in order:
            to = group_at(k)
            for m in range(PIECE):
                send[k - 1, piece * PIECE + m] = rows[within(idx_s[to, piece * PIECE + m], ROWS)]
            data_copy(k, piece * PIECE, PIECE).start()

    pack(0, SEND_ORDER[0])
    for s, part in ((2, last), (6, last), (4, last), (2, first), (6, second), (2, second), (6, first),
                    (1, last), (1, first), (1, second)):
        start(s, part)

    nb = jnp.bitwise_and(jnp.right_shift(rid, 2), 7)
    t = jnp.bitwise_and(jnp.right_shift(nb, 1) - y, 3) * 2 + jnp.bitwise_and(nb + core, 1)
    r = t * REG + jnp.bitwise_and(rid, 3)
    of_region = onehot(WIDE * GROUP, g * GROUP + r).astype(BF16)
    a = jnp.sum(of_region.astype(F32) * dot(of_region, before), axis=0, keepdims=True)
    a_int = a.astype(I32)
    slot = onehot(128, a_int * GROUP + r).astype(BF16)
    position = nt((of_group * jnp.minimum(p, CAP - 1.0)).astype(BF16), slot)
    over = (jnp.max(p, axis=1, keepdims=True) >= CAP).astype(F32)
    position = jnp.where(lax.broadcasted_iota(I32, (WIDE, 128), 1) == FLAG, over, position)
    gaps = spacing[...].astype(F32)
    gaps = jnp.concatenate([gaps * (1.0 - a), gaps * a, jnp.zeros((128 - 2 * SAMP, ROWS), F32)], axis=0).astype(BF16)
    meta_s[...] = nt(of_region, gaps).astype(BF16).reshape(WIDE, GROUP, 128)
    for w in range(WIDE):
        pos_t[w] = position[w:w + 1].astype(I32)
    meta_r[0] = meta_s[wide]
    pos_v[0] = pos_t[wide]
    metas = {k: remote(meta_s.at[group_at(k)], meta_r.at[k], meta_ss.at[k], meta_rs.at[k], wide_at(k))
             for k in range(1, WIDE)}
    places = {k: remote(pos_t.at[group_at(k)], pos_v.at[k], pos_ss.at[k], pos_rs.at[k], wide_at(k))
              for k in range(1, WIDE)}
    for k in range(1, WIDE):
        metas[k].start()
        places[k].start()

    def pack_all(order, begin=0):
        def step(piece, carry):
            pack(piece, order)
            return carry

        lax.fori_loop(begin, CAP // PIECE, step, 0)

    for i, order in enumerate(SEND_ORDER):
        pack_all(order, 1 if i == 0 else 0)

    def pack_own(piece, carry):
        q, s = place[0]
        for m in range(PIECE):
            recv[q][s * CAP + piece * PIECE + m] = rows[within(idx_s[wide, piece * PIECE + m], ROWS)]
        return carry

    lax.fori_loop(0, CAP // PIECE, pack_own, 0)

    offset = jnp.bitwise_and(way * (jnp.right_shift(g, 2) - z), 3) * 4 + jnp.bitwise_and(way * (jnp.bitwise_and(g, 3) - x), 3)
    came = onehot(2 * WIDE, offset * 2 + a_int).astype(F32)
    where_row[...] = jnp.concatenate([came, came], axis=0).astype(BF16)
    keep[...] = onehot(GROUP, r).astype(F32)
    line = lax.broadcasted_iota(I32, (MOST, MOST), 0)
    lane = lax.broadcasted_iota(I32, (MOST, MOST), 1)
    same = jnp.zeros((MOST, MOST), jnp.bool_)
    for b in range(MOST // SAMP):
        ends = (b * SAMP, (b + 1) * SAMP)
        same = jnp.logical_or(same, jnp.logical_and(jnp.logical_and(line >= ends[0], line < ends[1]),
                                                    jnp.logical_and(lane >= ends[0], lane < ends[1])))
    earlier[...] = jnp.logical_and(same, line < lane).astype(BF16)
    line = lax.broadcasted_iota(I32, (16, MOST), 0)
    lane = lax.broadcasted_iota(I32, (16, MOST), 1)
    pick[...] = jnp.logical_and(lane >= line * SAMP, lane < (line + 1) * SAMP).astype(BF16)

    for k in range(1, WIDE):
        metas[k].wait_recv()
        places[k].wait_recv()
    to_smem = pltpu.make_async_copy(pos_v, pos_s, local_sem.at[8])
    to_smem.start()
    flag = pos_v[0]
    for k in range(1, WIDE):
        flag = jnp.maximum(flag, pos_v[k])
    flag_s[...] = flag
    flags = {s: remote(flag_s, flag_r.at[s], flag_ss.at[s], flag_rs.at[s], narrow_at(s // 2, s % 2))
             for s in range(1, NARROW)}
    for copy in flags.values():
        copy.start()

    for s in (2, 6, 4):
        arrived(s, last)
        start(s + 1, last)
    own_weights[2].wait()
    for s in (1, 3, 7, 5):
        arrived(s, last)

    def spread(s, carry):
        lanes = lax.broadcasted_iota(I32, (REG * 4, 128), 1)
        line = lax.broadcasted_iota(I32, (REG * 4, 128), 0)
        channel = jnp.bitwise_and(line, 3)
        heads = wo[s].astype(F32).reshape(REG * 4, HID).astype(BF16)
        for j in range(REG):
            match = jnp.logical_and(jnp.right_shift(line, 2) == j, lanes == channel * GROUP + s * REG + j)
            wp[pl.ds((s * REG + j) * HID, HID)] = tn(heads, match.astype(BF16)).astype(BF16)
        return carry

    lax.fori_loop(0, NARROW, spread, 0)

    arrived(2, first), start(4, first), start(3, first)
    arrived(6, second), start(4, second), start(7, second)
    arrived(2, second), start(3, second)
    arrived(6, first), start(7, first)
    own_weights[0].wait(), own_weights[1].wait()
    for part in (first, second):
        arrived(1, part)
    to_smem.wait()

    returns = {}
    for q, chunk in enumerate(CHUNKS):
        size = len(chunk) * 2 * SAMP
        for k in chunk:
            if k:
                data_copy(k, 0, CAP).wait_recv()
        for order in HELD.get(q, ()):
            pack_all(order)
        acc[...] = jnp.zeros_like(acc)

        def regions(i, carry, q=q, chunk=chunk, size=size):
            dy = i + (i // 2) * (1 - 2 * (i % 2))
            if q == 0:
                @pl.when(i == 1)
                def _():
                    arrived(3, first), arrived(3, second)

                @pl.when(i == 2)
                def _():
                    arrived(4, first), start(5, first)
                    arrived(4, second), start(5, second)
                    arrived(7, first), arrived(7, second)

                @pl.when(i == 3)
                def _():
                    arrived(5, first), arrived(5, second)

            def rows_of(j):
                return jnp.concatenate(
                    [recv[q][s * CAP + within(pos_s[k, 0, ahead * GROUP + dy * 2 * REG + j], CAP)]
                     for s, k in enumerate(chunk) for ahead in range(2)], axis=0)

            span = range(2 * REG)
            hidden = [relu(dot(rows_of(j), wi[dy * 2 * REG + j])) for j in span]
            hidden = [relu(dot(hidden[j], wm[dy * 2 * REG + j, 0])) for j in span]
            hidden = [relu(dot(hidden[j], wm[dy * 2 * REG + j, 1])) for j in span]
            acc[0:size] += dot(jnp.concatenate(hidden, axis=1), wp[pl.ds(dy * 2 * REG * HID, 2 * REG * HID)])
            return carry

        lax.fori_loop(0, NARROW // 2, regions, 0)

        raw = acc[0:size].T
        gap = jnp.concatenate([meta_r[k, :, 0:2 * SAMP].astype(F32) for k in chunk], axis=1)
        density = raw[0:GROUP]
        density = jnp.maximum(density, 0.0) + jnp.log1p(jnp.exp(-jnp.abs(density)))
        optical = density * gap
        sums = dot(halves(optical), earlier[0:size, 0:size])
        passed = jnp.exp(-(sums[0:GROUP] + sums[GROUP:2 * GROUP]))
        series = optical * (1.0 - optical * (1 / 2 - optical * (1 / 6 - optical * (1 / 24 - optical * (1 / 120)))))
        weight = passed * jnp.where(optical < 0.125, series, 1.0 - jnp.exp(-optical))
        parts = [weight * jax.nn.sigmoid(raw[(c + 1) * GROUP:(c + 2) * GROUP]) for c in range(3)] + [optical]
        result = nt(pick[:, 0:size], halves(jnp.concatenate(parts, axis=0)))
        result = result[:, 0:128] + result[:, 128:256]
        for s, k in enumerate(chunk):
            target = ret_s if k else ret_r
            target[k] = result[2 * s:2 * s + 2]
            if k:
                returns[k] = remote(ret_s.at[k], ret_r.at[k], ret_ss.at[k], ret_rs.at[k], wide_at(k, -1))
                returns[k].start()

    for k in range(1, WIDE):
        returns[k].wait_recv()
    back = jnp.concatenate([ret_r[k] for k in range(WIDE)], axis=0)
    found = tn(halves(back), where_row[...])
    for c in range(4):
        fin_s[c:c + 1, :] = jnp.sum(found[c * GROUP:(c + 1) * GROUP] * keep[...], axis=0, keepdims=True)
    finals = {k: remote(fin_s, fin_r.at[wide], fin_ss.at[k], fin_rs.at[k], wide_at(k)) for k in range(1, WIDE)}
    for copy in finals.values():
        copy.start()
    fin_r[wide] = fin_s[...]
    for s in range(1, NARROW):
        flags[s].wait_recv()
        flag = jnp.maximum(flag, flag_r[s])
    over_out[...] = jnp.broadcast_to(flag[:, FLAG:FLAG + 1], (1, 128))
    for s in range(1, NARROW):
        for copy in weights[s]:
            copy.wait_send()
        flags[s].wait_send()
    for k in range(1, WIDE):
        metas[k].wait_send()
        places[k].wait_send()
        data_copy(k, 0, CAP).wait_send()
        returns[k].wait_send()
    for k in range(1, WIDE):
        remote(fin_s, fin_r.at[group_at(k, -1)], fin_ss.at[k], fin_rs.at[k], wide_at(k)).wait_recv()

    depth = [fin_r[s, 3:4, :] for s in range(WIDE)]
    ahead, behind = [jnp.zeros_like(depth[0])], [jnp.zeros_like(depth[0])]
    for s in range(WIDE - 1):
        ahead.append(ahead[-1] + depth[s])
        behind.append(behind[-1] + depth[WIDE - 1 - s])
    backward = dirs[...] == 1
    colour = jnp.zeros((3, ROWS), F32)
    for s in range(WIDE):
        light = jnp.exp(-jnp.where(backward, behind[WIDE - 1 - s], ahead[s]))
        colour = colour + light * fin_r[s, 0:3, :]
    out[...] = colour
    for k in range(1, WIDE):
        finals[k].wait_send()


def render(samples, spacing, ids, dirs, w_in, w_mid, w_out):
    vmem, smem, dma = pltpu.VMEM, pltpu.SMEM, pltpu.SemaphoreType.DMA
    regions = NARROW * REG
    whole, any_place = pl.BlockSpec(memory_space=pltpu.VMEM), pl.BlockSpec(memory_space=pl.ANY)
    scratch = [vmem((ROWS, SAMP, FEAT), BF16), vmem((WIDE - 1, CAP, SAMP, FEAT), BF16)]
    scratch += [vmem((len(chunk) * CAP, SAMP, FEAT), BF16) for chunk in CHUNKS]
    scratch += [
        vmem((regions, FEAT, HID), BF16), vmem((regions, 2, HID, HID), BF16), vmem((NARROW, REG, 4, HID), BF16),
        vmem((regions * HID, 128), BF16), vmem((WIDE, GROUP, 128), BF16), vmem((WIDE, GROUP, 128), BF16),
        vmem((WIDE, 1, 128), I32), vmem((WIDE, 1, 128), I32), smem((WIDE, 1, 128), I32), vmem((WIDE, 128), I32), smem((WIDE, 128), I32),
        vmem((MOST, 128), F32), vmem((MOST, MOST), BF16), vmem((16, MOST), BF16), vmem((4 * WIDE, ROWS), BF16),
        vmem((GROUP, ROWS), F32), vmem((WIDE, 2, 128), F32), vmem((WIDE, 2, 128), F32),
        vmem((4, ROWS), F32), vmem((WIDE, 4, ROWS), F32), vmem((1, 128), I32), vmem((NARROW, 1, 128), I32),
        dma((9,)), dma((5, NARROW)), dma((5, NARROW)), dma((WIDE,)), dma((WIDE,)), dma((WIDE,)), dma((WIDE,)), dma((WIDE,)),
        dma((WIDE,)), dma((WIDE,)), dma((WIDE,)), dma((WIDE,)), dma((WIDE,)), dma((NARROW,)), dma((NARROW,))]
    return pl.pallas_call(
        render_kernel,
        out_shape=(jax.ShapeDtypeStruct((3, ROWS), F32), jax.ShapeDtypeStruct((1, 128), I32)),
        in_specs=[any_place, whole, whole, whole, any_place, any_place, any_place],
        out_specs=(whole, whole),
        scratch_shapes=scratch,
        compiler_params=pltpu.CompilerParams(collective_id=0, has_side_effects=True, vmem_limit_bytes=58 * 2**20),
        name="render",
    )(samples, spacing, ids, dirs, w_in, w_mid, w_out)


def on_device(samples, spacing, region_ids, directions, w_in, w_mid, w_out):
    args = (samples, spacing, region_ids, directions, w_in, w_mid, w_out)
    fast, over = render(
        samples.reshape(ROWS, SAMP, FEAT), spacing.reshape(ROWS, SAMP).T, region_ids.reshape(1, ROWS),
        directions.reshape(1, ROWS), w_in, w_mid, w_out)
    return lax.cond(over[0, 0] > 0, lambda rest: general(*rest), lambda rest: fast, args)


def solution(mesh):
    in_specs = (
        P("wide", "narrow", None, None),
        P("wide", "narrow", None),
        P("wide", "narrow", None),
        P("narrow"),
        P(("wide", "narrow"), None, None),
        P(("wide", "narrow"), None, None, None),
        P(("wide", "narrow"), None, None),
    )
    out_specs = P(None, "narrow")
    return jax.shard_map(
        on_device, mesh=mesh, in_specs=in_specs, out_specs=out_specs, check_vma=False
    )
```

```python
import jax
import jax.numpy as jnp
from jax import lax
from jax.experimental import pallas as pl
from jax.experimental.pallas import tpu as pltpu
from jax.sharding import PartitionSpec as P

MESH = pl.DeviceIdType.MESH
F32, BF16, I32 = jnp.float32, jnp.bfloat16, jnp.int32
ROWS, SAMP, FEAT, HID = 512, 48, 128, 256
WIDE, NARROW, REG, GROUP = 16, 8, 4, 32
CAP = 40
PIECE = 4
FLAG = 127

SEND_ORDER = ((6, 14, 9, 11, 1, 3, 4, 12), (2, 8, 10))
HELD = {0: ((5, 15),), 1: ((7, 13),)}
CHUNKS = ((0, 6, 14, 9), (11, 1, 3, 4), (12, 2, 8, 10), (5, 15), (7, 13))
MOST = 4 * 2 * SAMP


def nt(a, b):
    return lax.dot_general(a, b, (((1,), (1,)), ((), ())), preferred_element_type=F32)


def tn(a, b):
    return lax.dot_general(a, b, (((0,), (0,)), ((), ())), preferred_element_type=F32)


def dot(a, b):
    return jnp.dot(a, b, preferred_element_type=F32)


def halves(v):
    high = v.astype(BF16)
    return jnp.concatenate([high, (v - high.astype(F32)).astype(BF16)], axis=0)


def onehot(rows, lanes_value):
    return lax.broadcasted_iota(I32, (rows, lanes_value.shape[1]), 0) == lanes_value


def within(i, size):
    return jnp.minimum(jnp.maximum(i, 0), size - 1)


def relu(v):
    return jnp.maximum(v.astype(BF16), 0)


def prefix_2(array, axis, combine, identity, reverse):
    count, position = (lax.axis_size(axis), lax.axis_index(axis))
    everything = lax.all_gather(array, axis)
    start = jnp.broadcast_to(jnp.asarray(identity, array.dtype), array.shape)

    def hop(k, before):
        at = count - 1 - k if reverse else k
        reached = at > position if reverse else at < position
        new = combine(before, everything[at])
        return jnp.where(reached, new, before)

    return lax.fori_loop(0, count, hop, start)


def composite(raw_out, spacing_part):
    density = jax.nn.softplus(raw_out[0])
    colours = jax.nn.sigmoid(raw_out[1:4])
    optical = density * spacing_part.astype(jnp.float32)
    before_sum = jnp.cumsum(optical, axis=-1) - optical
    sample_weight = jnp.exp(-before_sum) * -jnp.expm1(-optical)
    seg_colour = jnp.sum(sample_weight * colours, axis=-1)
    seg_depth = jnp.sum(optical, axis=-1)
    return jnp.stack([seg_colour[0], seg_colour[1], seg_colour[2], seg_depth], axis=-1)


def accumulate(earlier, later):
    return earlier + later


def general(samples, spacing, region_ids, directions, w_in, w_mid, w_out):
    wide_size = lax.axis_size("wide")
    narrow_size = lax.axis_size("narrow")
    devices_all = wide_size * narrow_size
    reg_local = w_in.shape[0]
    ray_local = samples.shape[1]
    sample_len = samples.shape[2]
    width_in = samples.shape[3]
    region_all = reg_local * devices_all
    capacity = max(2, 2 * ray_local // region_all)
    slot_total = region_all * capacity
    region_row = region_ids.reshape(ray_local)
    matches = region_row[:, None] == region_row[None, :]
    positions = jnp.arange(ray_local, dtype=jnp.int32)
    earlier = positions[None, :] < positions[:, None]
    arrival = jnp.sum(jnp.logical_and(matches, earlier), axis=1)
    slot_index = region_row * capacity + arrival
    source_row = jnp.full((slot_total,), ray_local, jnp.int32).at[slot_index].set(positions)
    ray_rows = jnp.concatenate(
        [
            samples.reshape(ray_local, sample_len, width_in),
            jnp.zeros((1, sample_len, width_in), samples.dtype),
        ],
        axis=0,
    )
    gap_rows = jnp.concatenate(
        [spacing.reshape(ray_local, sample_len), jnp.zeros((1, sample_len), spacing.dtype)], axis=0
    )
    send_features = jnp.take(ray_rows, source_row, axis=0)
    send_spacing = jnp.take(gap_rows, source_row, axis=0)
    features = lax.all_to_all(
        send_features.reshape(devices_all, reg_local, capacity, sample_len, width_in),
        ("wide", "narrow"),
        split_axis=0,
        concat_axis=0,
        tiled=True,
    )
    spacing_part = lax.all_to_all(
        send_spacing.reshape(devices_all, reg_local, capacity, sample_len),
        ("wide", "narrow"),
        split_axis=0,
        concat_axis=0,
        tiled=True,
    )
    results = []
    for region in range(reg_local):
        inputs = features[:, region].reshape(-1, width_in)
        hidden = jax.nn.relu(
            jnp.dot(inputs, w_in[region], preferred_element_type=jnp.float32)
        ).astype(jnp.bfloat16)
        for layer_index in range(w_mid.shape[1]):
            hidden = jax.nn.relu(
                jnp.dot(hidden, w_mid[region, layer_index], preferred_element_type=jnp.float32)
            ).astype(jnp.bfloat16)
        raw_out = jnp.einsum("nh,ch->cn", hidden, w_out[region], preferred_element_type=jnp.float32)
        part_gap = spacing_part[:, region]
        raw_out = raw_out.reshape((4,) + part_gap.shape)
        results.append(composite(raw_out, part_gap))
    partial_here = jnp.stack(results, axis=1)
    returned = lax.all_to_all(
        partial_here, ("wide", "narrow"), split_axis=0, concat_axis=0, tiled=True
    )
    mine = jnp.take(returned.reshape(slot_total, 4), slot_index, axis=0)
    seg_depth = mine[:, 3]
    zero_depth = jnp.zeros_like(seg_depth)
    ahead = prefix_2(seg_depth, "wide", accumulate, zero_depth, False)
    behind = prefix_2(seg_depth, "wide", accumulate, zero_depth, True)
    prefix = jnp.where(directions == 1, behind, ahead)
    light = jnp.exp(-prefix)
    light_term = (light[:, None] * mine[:, :3]).T
    return lax.psum(light_term, "wide")


def render_kernel(samples, spacing, ids, dirs, w_in, w_mid, w_out, out, over_out, *scratch):
    rows, send, *recv = scratch[0:2 + len(CHUNKS)]
    (wi, wm, wo, wp, meta_s, meta_r, pos_t, pos_v, pos_s, idx_v, idx_s, acc,
     earlier, pick, where_row, keep, ret_s, ret_r, fin_s, fin_r, flag_s, flag_r, local_sem, wt_send, wt_recv,
     meta_ss, meta_rs, pos_ss, pos_rs, data_ss, data_rs, ret_ss, ret_rs, fin_ss, fin_rs, flag_ss, flag_rs) = scratch[2 + len(CHUNKS):]
    place = {k: (q, s) for q, chunk in enumerate(CHUNKS) for s, k in enumerate(chunk)}
    wide, nar = lax.axis_index("wide"), lax.axis_index("narrow")
    z, x = wide // 4, wide % 4
    y, core = nar // 2, nar % 2

    way = 1 - 2 * core

    def group_at(k, sign=1):
        return ((z + sign * way * (k // 4) + 4) % 4) * 4 + (x + sign * way * (k % 4) + 4) % 4

    def wide_at(k, sign=1):
        return (group_at(k, sign), nar)

    def narrow_at(dy, dc):
        return (wide, ((y + dy + 4) % 4) * 2 + (core + dc) % 2)

    def remote(src, dst, ss, rs, to):
        return pltpu.make_async_remote_copy(
            src_ref=src, dst_ref=dst, send_sem=ss, recv_sem=rs, device_id=to, device_id_type=MESH)

    barrier = pltpu.get_barrier_semaphore()
    for k in range(1, WIDE):
        pl.semaphore_signal(barrier, inc=1, device_id=wide_at(k), device_id_type=MESH)
    for t in range(1, NARROW):
        pl.semaphore_signal(barrier, inc=1, device_id=narrow_at(t // 2, t % 2), device_id_type=MESH)

    quarter = ROWS // 4
    own_rows = [pltpu.make_async_copy(samples.at[pl.ds(i * quarter, quarter)], rows.at[pl.ds(i * quarter, quarter)],
                                      local_sem.at[i]) for i in range(4)]
    own_weights = [pltpu.make_async_copy(w_in, wi.at[pl.ds(0, REG)], local_sem.at[4]),
                   pltpu.make_async_copy(w_mid, wm.at[pl.ds(0, REG)], local_sem.at[5]),
                   pltpu.make_async_copy(w_out, wo.at[0], local_sem.at[6])]
    for copy in own_rows + own_weights:
        copy.start()

    rid = ids[...]
    g = jnp.right_shift(rid, 5)
    ray = lax.broadcasted_iota(I32, (1, ROWS), 1)
    before = (lax.broadcasted_iota(I32, (ROWS, ROWS), 0) < lax.broadcasted_iota(I32, (ROWS, ROWS), 1)).astype(BF16)
    of_group = onehot(WIDE, g).astype(F32)
    p = jnp.sum(of_group * dot(of_group.astype(BF16), before), axis=0, keepdims=True)
    at_place = onehot(128, p.astype(I32)).astype(BF16)
    low = of_group * jnp.bitwise_and(ray, 15).astype(F32)
    high = of_group * jnp.right_shift(ray, 4).astype(F32)
    source = nt(jnp.concatenate([low, high], axis=0).astype(BF16), at_place)
    idx_v[...] = (source[0:WIDE] + 16.0 * source[WIDE:2 * WIDE]).astype(I32)
    to_smem = pltpu.make_async_copy(idx_v, idx_s, local_sem.at[7])
    to_smem.start()

    pl.semaphore_wait(barrier, WIDE - 1 + NARROW - 1)

    half = REG // 2

    def weight_copies(s, to, taken_from=None):
        copies = []
        for h in range(2):
            for ref, own in ((wi, w_in), (wm, w_mid)):
                src = own.at[pl.ds(h * half, half)] if taken_from is None else ref.at[pl.ds(taken_from * REG + h * half, half)]
                i = 2 * h + (0 if ref is wi else 1)
                copies.append(remote(src, ref.at[pl.ds(s * REG + h * half, half)], wt_send.at[i, s], wt_recv.at[i, s], to))
        src = w_out if taken_from is None else wo.at[taken_from]
        return copies + [remote(src, wo.at[s], wt_send.at[4, s], wt_recv.at[4, s], to)]

    weights = {1: weight_copies(1, narrow_at(0, 1)), 2: weight_copies(2, narrow_at(-1, 0)),
               6: weight_copies(6, narrow_at(1, 0)), 3: weight_copies(3, narrow_at(0, 1), 2),
               7: weight_copies(7, narrow_at(0, 1), 6), 5: weight_copies(5, narrow_at(0, 1), 4)}
    weights[4] = weight_copies(4, narrow_at(-1, 0), 2)[0:2] + weight_copies(4, narrow_at(1, 0), 6)[2:4]
    weights[4] += weight_copies(4, narrow_at(2, 0))[4:5]
    first, second, last = slice(0, 2), slice(2, 4), slice(4, 5)

    def start(s, part):
        for copy in weights[s][part]:
            copy.start()

    def arrived(s, part):
        for copy in weights[s][part]:
            copy.wait_recv()

    for copy in own_rows:
        copy.wait()
    to_smem.wait()

    def data_copy(k, begin, size):
        q, s = place[k]
        return remote(send.at[k - 1, pl.ds(begin, size)], recv[q].at[pl.ds(s * CAP + begin, size)],
                      data_ss.at[k], data_rs.at[k], wide_at(k))

    def pack(piece, order):
        for k in order:
            to = group_at(k)
            for m in range(PIECE):
                send[k - 1, piece * PIECE + m] = rows[within(idx_s[to, piece * PIECE + m], ROWS)]
            data_copy(k, piece * PIECE, PIECE).start()

    pack(0, SEND_ORDER[0])
    for s, part in ((2, last), (6, last), (4, last), (2, first), (6, second), (2, second), (6, first),
                    (1, last), (1, first), (1, second)):
        start(s, part)

    nb = jnp.bitwise_and(jnp.right_shift(rid, 2), 7)
    t = jnp.bitwise_and(jnp.right_shift(nb, 1) - y, 3) * 2 + jnp.bitwise_and(nb + core, 1)
    r = t * REG + jnp.bitwise_and(rid, 3)
    of_region = onehot(WIDE * GROUP, g * GROUP + r).astype(BF16)
    a = jnp.sum(of_region.astype(F32) * dot(of_region, before), axis=0, keepdims=True)
    a_int = a.astype(I32)
    slot = onehot(128, a_int * GROUP + r).astype(BF16)
    position = nt((of_group * jnp.minimum(p, CAP - 1.0)).astype(BF16), slot)
    over = (jnp.max(p, axis=1, keepdims=True) >= CAP).astype(F32)
    position = jnp.where(lax.broadcasted_iota(I32, (WIDE, 128), 1) == FLAG, over, position)
    gaps = spacing[...].astype(F32)
    gaps = jnp.concatenate([gaps * (1.0 - a), gaps * a, jnp.zeros((128 - 2 * SAMP, ROWS), F32)], axis=0).astype(BF16)
    meta_s[...] = nt(of_region, gaps).astype(BF16).reshape(WIDE, GROUP, 128)
    for w in range(WIDE):
        pos_t[w] = position[w:w + 1].astype(I32)
    meta_r[0] = meta_s[wide]
    pos_v[0] = pos_t[wide]
    metas = {k: remote(meta_s.at[group_at(k)], meta_r.at[k], meta_ss.at[k], meta_rs.at[k], wide_at(k))
             for k in range(1, WIDE)}
    places = {k: remote(pos_t.at[group_at(k)], pos_v.at[k], pos_ss.at[k], pos_rs.at[k], wide_at(k))
              for k in range(1, WIDE)}
    for k in range(1, WIDE):
        metas[k].start()
        places[k].start()

    def pack_all(order, begin=0):
        def step(piece, carry):
            pack(piece, order)
            return carry

        lax.fori_loop(begin, CAP // PIECE, step, 0)

    for i, order in enumerate(SEND_ORDER):
        pack_all(order, 1 if i == 0 else 0)

    def pack_own(piece, carry):
        q, s = place[0]
        for m in range(PIECE):
            recv[q][s * CAP + piece * PIECE + m] = rows[within(idx_s[wide, piece * PIECE + m], ROWS)]
        return carry

    lax.fori_loop(0, CAP // PIECE, pack_own, 0)

    offset = jnp.bitwise_and(way * (jnp.right_shift(g, 2) - z), 3) * 4 + jnp.bitwise_and(way * (jnp.bitwise_and(g, 3) - x), 3)
    came = onehot(2 * WIDE, offset * 2 + a_int).astype(F32)
    where_row[...] = jnp.concatenate([came, came], axis=0).astype(BF16)
    keep[...] = onehot(GROUP, r).astype(F32)
    line = lax.broadcasted_iota(I32, (MOST, MOST), 0)
    lane = lax.broadcasted_iota(I32, (MOST, MOST), 1)
    same = jnp.zeros((MOST, MOST), jnp.bool_)
    for b in range(MOST // SAMP):
        ends = (b * SAMP, (b + 1) * SAMP)
        same = jnp.logical_or(same, jnp.logical_and(jnp.logical_and(line >= ends[0], line < ends[1]),
                                                    jnp.logical_and(lane >= ends[0], lane < ends[1])))
    earlier[...] = jnp.logical_and(same, line < lane).astype(BF16)
    line = lax.broadcasted_iota(I32, (16, MOST), 0)
    lane = lax.broadcasted_iota(I32, (16, MOST), 1)
    pick[...] = jnp.logical_and(lane >= line * SAMP, lane < (line + 1) * SAMP).astype(BF16)

    for k in range(1, WIDE):
        metas[k].wait_recv()
        places[k].wait_recv()
    to_smem = pltpu.make_async_copy(pos_v, pos_s, local_sem.at[8])
    to_smem.start()
    flag = pos_v[0]
    for k in range(1, WIDE):
        flag = jnp.maximum(flag, pos_v[k])
    flag_s[...] = flag
    flags = {s: remote(flag_s, flag_r.at[s], flag_ss.at[s], flag_rs.at[s], narrow_at(s // 2, s % 2))
             for s in range(1, NARROW)}
    for copy in flags.values():
        copy.start()

    for s in (2, 6, 4):
        arrived(s, last)
        start(s + 1, last)
    own_weights[2].wait()
    for s in (1, 3, 7, 5):
        arrived(s, last)

    def spread(s, carry):
        lanes = lax.broadcasted_iota(I32, (REG * 4, 128), 1)
        line = lax.broadcasted_iota(I32, (REG * 4, 128), 0)
        channel = jnp.bitwise_and(line, 3)
        heads = wo[s].astype(F32).reshape(REG * 4, HID).astype(BF16)
        for j in range(REG):
            match = jnp.logical_and(jnp.right_shift(line, 2) == j, lanes == channel * GROUP + s * REG + j)
            wp[pl.ds((s * REG + j) * HID, HID)] = tn(heads, match.astype(BF16)).astype(BF16)
        return carry

    lax.fori_loop(0, NARROW, spread, 0)

    arrived(2, first), start(4, first), start(3, first)
    arrived(6, second), start(4, second), start(7, second)
    arrived(2, second), start(3, second)
    arrived(6, first), start(7, first)
    own_weights[0].wait(), own_weights[1].wait()
    for part in (first, second):
        arrived(1, part)
    to_smem.wait()

    returns = {}
    for q, chunk in enumerate(CHUNKS):
        size = len(chunk) * 2 * SAMP
        for k in chunk:
            if k:
                data_copy(k, 0, CAP).wait_recv()
        for order in HELD.get(q, ()):
            pack_all(order)
        acc[...] = jnp.zeros_like(acc)

        def regions(i, carry, q=q, chunk=chunk, size=size):
            dy = i + (i // 2) * (1 - 2 * (i % 2))
            if q == 0:
                @pl.when(i == 1)
                def _():
                    arrived(3, first), arrived(3, second)

                @pl.when(i == 2)
                def _():
                    arrived(4, first), start(5, first)
                    arrived(4, second), start(5, second)
                    arrived(7, first), arrived(7, second)

                @pl.when(i == 3)
                def _():
                    arrived(5, first), arrived(5, second)

            def rows_of(j):
                return jnp.concatenate(
                    [recv[q][s * CAP + within(pos_s[k, 0, ahead * GROUP + dy * 2 * REG + j], CAP)]
                     for s, k in enumerate(chunk) for ahead in range(2)], axis=0)

            span = range(2 * REG)
            hidden = [relu(dot(rows_of(j), wi[dy * 2 * REG + j])) for j in span]
            hidden = [relu(dot(hidden[j], wm[dy * 2 * REG + j, 0])) for j in span]
            hidden = [relu(dot(hidden[j], wm[dy * 2 * REG + j, 1])) for j in span]
            acc[0:size] += dot(jnp.concatenate(hidden, axis=1), wp[pl.ds(dy * 2 * REG * HID, 2 * REG * HID)])
            return carry

        lax.fori_loop(0, NARROW // 2, regions, 0)

        raw = acc[0:size].T
        gap = jnp.concatenate([meta_r[k, :, 0:2 * SAMP].astype(F32) for k in chunk], axis=1)
        density = raw[0:GROUP]
        density = jnp.maximum(density, 0.0) + jnp.log1p(jnp.exp(-jnp.abs(density)))
        optical = density * gap
        sums = dot(halves(optical), earlier[0:size, 0:size])
        passed = jnp.exp(-(sums[0:GROUP] + sums[GROUP:2 * GROUP]))
        series = optical * (1.0 - optical * (1 / 2 - optical * (1 / 6 - optical * (1 / 24 - optical * (1 / 120)))))
        weight = passed * jnp.where(optical < 0.125, series, 1.0 - jnp.exp(-optical))
        parts = [weight * jax.nn.sigmoid(raw[(c + 1) * GROUP:(c + 2) * GROUP]) for c in range(3)] + [optical]
        result = nt(pick[:, 0:size], halves(jnp.concatenate(parts, axis=0)))
        result = result[:, 0:128] + result[:, 128:256]
        for s, k in enumerate(chunk):
            target = ret_s if k else ret_r
            target[k] = result[2 * s:2 * s + 2]
            if k:
                returns[k] = remote(ret_s.at[k], ret_r.at[k], ret_ss.at[k], ret_rs.at[k], wide_at(k, -1))
                returns[k].start()

    for k in range(1, WIDE):
        returns[k].wait_recv()
    back = jnp.concatenate([ret_r[k] for k in range(WIDE)], axis=0)
    found = tn(halves(back), where_row[...])
    for c in range(4):
        fin_s[c:c + 1, :] = jnp.sum(found[c * GROUP:(c + 1) * GROUP] * keep[...], axis=0, keepdims=True)
    finals = {k: remote(fin_s, fin_r.at[wide], fin_ss.at[k], fin_rs.at[k], wide_at(k)) for k in range(1, WIDE)}
    for copy in finals.values():
        copy.start()
    fin_r[wide] = fin_s[...]
    for s in range(1, NARROW):
        flags[s].wait_recv()
        flag = jnp.maximum(flag, flag_r[s])
    over_out[...] = jnp.broadcast_to(flag[:, FLAG:FLAG + 1], (1, 128))
    for s in range(1, NARROW):
        for copy in weights[s]:
            copy.wait_send()
        flags[s].wait_send()
    for k in range(1, WIDE):
        metas[k].wait_send()
        places[k].wait_send()
        data_copy(k, 0, CAP).wait_send()
        returns[k].wait_send()
    for k in range(1, WIDE):
        remote(fin_s, fin_r.at[group_at(k, -1)], fin_ss.at[k], fin_rs.at[k], wide_at(k)).wait_recv()

    depth = [fin_r[s, 3:4, :] for s in range(WIDE)]
    ahead, behind = [jnp.zeros_like(depth[0])], [jnp.zeros_like(depth[0])]
    for s in range(WIDE - 1):
        ahead.append(ahead[-1] + depth[s])
        behind.append(behind[-1] + depth[WIDE - 1 - s])
    backward = dirs[...] == 1
    colour = jnp.zeros((3, ROWS), F32)
    for s in range(WIDE):
        light = jnp.exp(-jnp.where(backward, behind[WIDE - 1 - s], ahead[s]))
        colour = colour + light * fin_r[s, 0:3, :]
    out[...] = colour
    for k in range(1, WIDE):
        finals[k].wait_send()


def render(samples, spacing, ids, dirs, w_in, w_mid, w_out):
    vmem, smem, dma = pltpu.VMEM, pltpu.SMEM, pltpu.SemaphoreType.DMA
    regions = NARROW * REG
    whole, any_place = pl.BlockSpec(memory_space=pltpu.VMEM), pl.BlockSpec(memory_space=pl.ANY)
    scratch = [vmem((ROWS, SAMP, FEAT), BF16), vmem((WIDE - 1, CAP, SAMP, FEAT), BF16)]
    scratch += [vmem((len(chunk) * CAP, SAMP, FEAT), BF16) for chunk in CHUNKS]
    scratch += [
        vmem((regions, FEAT, HID), BF16), vmem((regions, 2, HID, HID), BF16), vmem((NARROW, REG, 4, HID), BF16),
        vmem((regions * HID, 128), BF16), vmem((WIDE, GROUP, 128), BF16), vmem((WIDE, GROUP, 128), BF16),
        vmem((WIDE, 1, 128), I32), vmem((WIDE, 1, 128), I32), smem((WIDE, 1, 128), I32), vmem((WIDE, 128), I32), smem((WIDE, 128), I32),
        vmem((MOST, 128), F32), vmem((MOST, MOST), BF16), vmem((16, MOST), BF16), vmem((4 * WIDE, ROWS), BF16),
        vmem((GROUP, ROWS), F32), vmem((WIDE, 2, 128), F32), vmem((WIDE, 2, 128), F32),
        vmem((4, ROWS), F32), vmem((WIDE, 4, ROWS), F32), vmem((1, 128), I32), vmem((NARROW, 1, 128), I32),
        dma((9,)), dma((5, NARROW)), dma((5, NARROW)), dma((WIDE,)), dma((WIDE,)), dma((WIDE,)), dma((WIDE,)), dma((WIDE,)),
        dma((WIDE,)), dma((WIDE,)), dma((WIDE,)), dma((WIDE,)), dma((WIDE,)), dma((NARROW,)), dma((NARROW,))]
    return pl.pallas_call(
        render_kernel,
        out_shape=(jax.ShapeDtypeStruct((3, ROWS), F32), jax.ShapeDtypeStruct((1, 128), I32)),
        in_specs=[any_place, whole, whole, whole, any_place, any_place, any_place],
        out_specs=(whole, whole),
        scratch_shapes=scratch,
        compiler_params=pltpu.CompilerParams(collective_id=0, has_side_effects=True, vmem_limit_bytes=58 * 2**20),
        name="render",
    )(samples, spacing, ids, dirs, w_in, w_mid, w_out)


def on_device(samples, spacing, region_ids, directions, w_in, w_mid, w_out):
    args = (samples, spacing, region_ids, directions, w_in, w_mid, w_out)
    fast, over = render(
        samples.reshape(ROWS, SAMP, FEAT), spacing.reshape(ROWS, SAMP).T, region_ids.reshape(1, ROWS),
        directions.reshape(1, ROWS), w_in, w_mid, w_out)
    return lax.cond(over[0, 0] > 0, lambda rest: general(*rest), lambda rest: fast, args)


def solution(mesh):
    in_specs = (
        P("wide", "narrow", None, None),
        P("wide", "narrow", None),
        P("wide", "narrow", None),
        P("narrow"),
        P(("wide", "narrow"), None, None),
        P(("wide", "narrow"), None, None, None),
        P(("wide", "narrow"), None, None),
    )
    out_specs = P(None, "narrow")
    return jax.shard_map(
        on_device, mesh=mesh, in_specs=in_specs, out_specs=out_specs, check_vma=False
    )
```

```python
import jax
import jax.numpy as jnp
from jax import lax
from jax.experimental import pallas as pl
from jax.experimental.pallas import tpu as pltpu
from jax.sharding import PartitionSpec as P

MESH = pl.DeviceIdType.MESH
F32, BF16, I32 = jnp.float32, jnp.bfloat16, jnp.int32
ROWS, SAMP, FEAT, HID = 512, 48, 128, 256
WIDE, NARROW, REG, GROUP = 16, 8, 4, 32
CAP = 40
PIECE = 4
FLAG = 127

SEND_ORDER = ((6, 14, 9, 11, 1, 3, 4, 12), (2, 8, 10))
HELD = {0: ((5, 15),), 1: ((7, 13),)}
CHUNKS = ((0, 6, 14, 9), (11, 1, 3, 4), (12, 2, 8, 10), (5, 15), (7, 13))
MOST = 4 * 2 * SAMP


def nt(a, b):
    return lax.dot_general(a, b, (((1,), (1,)), ((), ())), preferred_element_type=F32)


def tn(a, b):
    return lax.dot_general(a, b, (((0,), (0,)), ((), ())), preferred_element_type=F32)


def dot(a, b):
    return jnp.dot(a, b, preferred_element_type=F32)


def halves(v):
    high = v.astype(BF16)
    return jnp.concatenate([high, (v - high.astype(F32)).astype(BF16)], axis=0)


def onehot(rows, lanes_value):
    return lax.broadcasted_iota(I32, (rows, lanes_value.shape[1]), 0) == lanes_value


def within(i, size):
    return jnp.minimum(jnp.maximum(i, 0), size - 1)


def relu(v):
    return jnp.maximum(v.astype(BF16), 0)


def prefix_2(array, axis, combine, identity, reverse):
    count, position = (lax.axis_size(axis), lax.axis_index(axis))
    everything = lax.all_gather(array, axis)
    start = jnp.broadcast_to(jnp.asarray(identity, array.dtype), array.shape)

    def hop(k, before):
        at = count - 1 - k if reverse else k
        reached = at > position if reverse else at < position
        new = combine(before, everything[at])
        return jnp.where(reached, new, before)

    return lax.fori_loop(0, count, hop, start)


def composite(raw_out, spacing_part):
    density = jax.nn.softplus(raw_out[0])
    colours = jax.nn.sigmoid(raw_out[1:4])
    optical = density * spacing_part.astype(jnp.float32)
    before_sum = jnp.cumsum(optical, axis=-1) - optical
    sample_weight = jnp.exp(-before_sum) * -jnp.expm1(-optical)
    seg_colour = jnp.sum(sample_weight * colours, axis=-1)
    seg_depth = jnp.sum(optical, axis=-1)
    return jnp.stack([seg_colour[0], seg_colour[1], seg_colour[2], seg_depth], axis=-1)


def accumulate(earlier, later):
    return earlier + later


def general(samples, spacing, region_ids, directions, w_in, w_mid, w_out):
    wide_size = lax.axis_size("wide")
    narrow_size = lax.axis_size("narrow")
    devices_all = wide_size * narrow_size
    reg_local = w_in.shape[0]
    ray_local = samples.shape[1]
    sample_len = samples.shape[2]
    width_in = samples.shape[3]
    region_all = reg_local * devices_all
    capacity = max(2, 2 * ray_local // region_all)
    slot_total = region_all * capacity
    region_row = region_ids.reshape(ray_local)
    matches = region_row[:, None] == region_row[None, :]
    positions = jnp.arange(ray_local, dtype=jnp.int32)
    earlier = positions[None, :] < positions[:, None]
    arrival = jnp.sum(jnp.logical_and(matches, earlier), axis=1)
    slot_index = region_row * capacity + arrival
    source_row = jnp.full((slot_total,), ray_local, jnp.int32).at[slot_index].set(positions)
    ray_rows = jnp.concatenate(
        [
            samples.reshape(ray_local, sample_len, width_in),
            jnp.zeros((1, sample_len, width_in), samples.dtype),
        ],
        axis=0,
    )
    gap_rows = jnp.concatenate(
        [spacing.reshape(ray_local, sample_len), jnp.zeros((1, sample_len), spacing.dtype)], axis=0
    )
    send_features = jnp.take(ray_rows, source_row, axis=0)
    send_spacing = jnp.take(gap_rows, source_row, axis=0)
    features = lax.all_to_all(
        send_features.reshape(devices_all, reg_local, capacity, sample_len, width_in),
        ("wide", "narrow"),
        split_axis=0,
        concat_axis=0,
        tiled=True,
    )
    spacing_part = lax.all_to_all(
        send_spacing.reshape(devices_all, reg_local, capacity, sample_len),
        ("wide", "narrow"),
        split_axis=0,
        concat_axis=0,
        tiled=True,
    )
    results = []
    for region in range(reg_local):
        inputs = features[:, region].reshape(-1, width_in)
        hidden = jax.nn.relu(
            jnp.dot(inputs, w_in[region], preferred_element_type=jnp.float32)
        ).astype(jnp.bfloat16)
        for layer_index in range(w_mid.shape[1]):
            hidden = jax.nn.relu(
                jnp.dot(hidden, w_mid[region, layer_index], preferred_element_type=jnp.float32)
            ).astype(jnp.bfloat16)
        raw_out = jnp.einsum("nh,ch->cn", hidden, w_out[region], preferred_element_type=jnp.float32)
        part_gap = spacing_part[:, region]
        raw_out = raw_out.reshape((4,) + part_gap.shape)
        results.append(composite(raw_out, part_gap))
    partial_here = jnp.stack(results, axis=1)
    returned = lax.all_to_all(
        partial_here, ("wide", "narrow"), split_axis=0, concat_axis=0, tiled=True
    )
    mine = jnp.take(returned.reshape(slot_total, 4), slot_index, axis=0)
    seg_depth = mine[:, 3]
    zero_depth = jnp.zeros_like(seg_depth)
    ahead = prefix_2(seg_depth, "wide", accumulate, zero_depth, False)
    behind = prefix_2(seg_depth, "wide", accumulate, zero_depth, True)
    prefix = jnp.where(directions == 1, behind, ahead)
    light = jnp.exp(-prefix)
    light_term = (light[:, None] * mine[:, :3]).T
    return lax.psum(light_term, "wide")


def render_kernel(samples, spacing, ids, dirs, w_in, w_mid, w_out, out, over_out, *scratch):
    rows, send, *recv = scratch[0:2 + len(CHUNKS)]
    (wi, wm, wo, wp, meta_s, meta_r, pos_t, pos_v, pos_s, idx_v, idx_s, acc,
     earlier, pick, where_row, keep, ret_s, ret_r, fin_s, fin_r, flag_s, flag_r, local_sem, wt_send, wt_recv,
     meta_ss, meta_rs, pos_ss, pos_rs, data_ss, data_rs, ret_ss, ret_rs, fin_ss, fin_rs, flag_ss, flag_rs) = scratch[2 + len(CHUNKS):]
    place = {k: (q, s) for q, chunk in enumerate(CHUNKS) for s, k in enumerate(chunk)}
    wide, nar = lax.axis_index("wide"), lax.axis_index("narrow")
    z, x = wide // 4, wide % 4
    y, core = nar // 2, nar % 2

    way = 1 - 2 * core

    def group_at(k, sign=1):
        return ((z + sign * way * (k // 4) + 4) % 4) * 4 + (x + sign * way * (k % 4) + 4) % 4

    def wide_at(k, sign=1):
        return (group_at(k, sign), nar)

    def narrow_at(dy, dc):
        return (wide, ((y + dy + 4) % 4) * 2 + (core + dc) % 2)

    def remote(src, dst, ss, rs, to):
        return pltpu.make_async_remote_copy(
            src_ref=src, dst_ref=dst, send_sem=ss, recv_sem=rs, device_id=to, device_id_type=MESH)

    barrier = pltpu.get_barrier_semaphore()
    for k in range(1, WIDE):
        pl.semaphore_signal(barrier, inc=1, device_id=wide_at(k), device_id_type=MESH)
    for t in range(1, NARROW):
        pl.semaphore_signal(barrier, inc=1, device_id=narrow_at(t // 2, t % 2), device_id_type=MESH)

    quarter = ROWS // 4
    own_rows = [pltpu.make_async_copy(samples.at[pl.ds(i * quarter, quarter)], rows.at[pl.ds(i * quarter, quarter)],
                                      local_sem.at[i]) for i in range(4)]
    own_weights = [pltpu.make_async_copy(w_in, wi.at[pl.ds(0, REG)], local_sem.at[4]),
                   pltpu.make_async_copy(w_mid, wm.at[pl.ds(0, REG)], local_sem.at[5]),
                   pltpu.make_async_copy(w_out, wo.at[0], local_sem.at[6])]
    for copy in own_rows + own_weights:
        copy.start()

    rid = ids[...]
    g = jnp.right_shift(rid, 5)
    ray = lax.broadcasted_iota(I32, (1, ROWS), 1)
    before = (lax.broadcasted_iota(I32, (ROWS, ROWS), 0) < lax.broadcasted_iota(I32, (ROWS, ROWS), 1)).astype(BF16)
    of_group = onehot(WIDE, g).astype(F32)
    p = jnp.sum(of_group * dot(of_group.astype(BF16), before), axis=0, keepdims=True)
    at_place = onehot(128, p.astype(I32)).astype(BF16)
    low = of_group * jnp.bitwise_and(ray, 15).astype(F32)
    high = of_group * jnp.right_shift(ray, 4).astype(F32)
    source = nt(jnp.concatenate([low, high], axis=0).astype(BF16), at_place)
    idx_v[...] = (source[0:WIDE] + 16.0 * source[WIDE:2 * WIDE]).astype(I32)
    to_smem = pltpu.make_async_copy(idx_v, idx_s, local_sem.at[7])
    to_smem.start()

    pl.semaphore_wait(barrier, WIDE - 1 + NARROW - 1)

    half = REG // 2

    def weight_copies(s, to, taken_from=None):
        copies = []
        for h in range(2):
            for ref, own in ((wi, w_in), (wm, w_mid)):
                src = own.at[pl.ds(h * half, half)] if taken_from is None else ref.at[pl.ds(taken_from * REG + h * half, half)]
                i = 2 * h + (0 if ref is wi else 1)
                copies.append(remote(src, ref.at[pl.ds(s * REG + h * half, half)], wt_send.at[i, s], wt_recv.at[i, s], to))
        src = w_out if taken_from is None else wo.at[taken_from]
        return copies + [remote(src, wo.at[s], wt_send.at[4, s], wt_recv.at[4, s], to)]

    weights = {1: weight_copies(1, narrow_at(0, 1)), 2: weight_copies(2, narrow_at(-1, 0)),
               6: weight_copies(6, narrow_at(1, 0)), 3: weight_copies(3, narrow_at(0, 1), 2),
               7: weight_copies(7, narrow_at(0, 1), 6), 5: weight_copies(5, narrow_at(0, 1), 4)}
    weights[4] = weight_copies(4, narrow_at(-1, 0), 2)[0:2] + weight_copies(4, narrow_at(1, 0), 6)[2:4]
    weights[4] += weight_copies(4, narrow_at(2, 0))[4:5]
    first, second, last = slice(0, 2), slice(2, 4), slice(4, 5)

    def start(s, part):
        for copy in weights[s][part]:
            copy.start()

    def arrived(s, part):
        for copy in weights[s][part]:
            copy.wait_recv()

    for copy in own_rows:
        copy.wait()
    to_smem.wait()

    def data_copy(k, begin, size):
        q, s = place[k]
        return remote(send.at[k - 1, pl.ds(begin, size)], recv[q].at[pl.ds(s * CAP + begin, size)],
                      data_ss.at[k], data_rs.at[k], wide_at(k))

    def pack(piece, order):
        for k in order:
            to = group_at(k)
            for m in range(PIECE):
                send[k - 1, piece * PIECE + m] = rows[within(idx_s[to, piece * PIECE + m], ROWS)]
            data_copy(k, piece * PIECE, PIECE).start()

    pack(0, SEND_ORDER[0])
    for s, part in ((2, last), (6, last), (4, last), (2, first), (6, second), (2, second), (6, first),
                    (1, last), (1, first), (1, second)):
        start(s, part)

    pack(1, SEND_ORDER[0])
    pack(2, SEND_ORDER[0])

    nb = jnp.bitwise_and(jnp.right_shift(rid, 2), 7)
    t = jnp.bitwise_and(jnp.right_shift(nb, 1) - y, 3) * 2 + jnp.bitwise_and(nb + core, 1)
    r = t * REG + jnp.bitwise_and(rid, 3)
    of_region = onehot(WIDE * GROUP, g * GROUP + r).astype(BF16)
    a = jnp.sum(of_region.astype(F32) * dot(of_region, before), axis=0, keepdims=True)
    a_int = a.astype(I32)
    slot = onehot(128, a_int * GROUP + r).astype(BF16)
    position = nt((of_group * jnp.minimum(p, CAP - 1.0)).astype(BF16), slot)
    over = (jnp.max(p, axis=1, keepdims=True) >= CAP).astype(F32)
    position = jnp.where(lax.broadcasted_iota(I32, (WIDE, 128), 1) == FLAG, over, position)
    gaps = spacing[...].astype(F32)
    gaps = jnp.concatenate([gaps * (1.0 - a), gaps * a, jnp.zeros((128 - 2 * SAMP, ROWS), F32)], axis=0).astype(BF16)
    meta_s[...] = nt(of_region, gaps).astype(BF16).reshape(WIDE, GROUP, 128)
    for w in range(WIDE):
        pos_t[w] = position[w:w + 1].astype(I32)
    meta_r[0] = meta_s[wide]
    pos_v[0] = pos_t[wide]
    metas = {k: remote(meta_s.at[group_at(k)], meta_r.at[k], meta_ss.at[k], meta_rs.at[k], wide_at(k))
             for k in range(1, WIDE)}
    places = {k: remote(pos_t.at[group_at(k)], pos_v.at[k], pos_ss.at[k], pos_rs.at[k], wide_at(k))
              for k in range(1, WIDE)}
    for k in range(1, WIDE):
        metas[k].start()
        places[k].start()

    def pack_all(order, begin=0):
        def step(piece, carry):
            pack(piece, order)
            return carry

        lax.fori_loop(begin, CAP // PIECE, step, 0)

    for i, order in enumerate(SEND_ORDER):
        pack_all(order, 3 if i == 0 else 0)

    def pack_own(piece, carry):
        q, s = place[0]
        for m in range(PIECE):
            recv[q][s * CAP + piece * PIECE + m] = rows[within(idx_s[wide, piece * PIECE + m], ROWS)]
        return carry

    lax.fori_loop(0, CAP // PIECE, pack_own, 0)

    offset = jnp.bitwise_and(way * (jnp.right_shift(g, 2) - z), 3) * 4 + jnp.bitwise_and(way * (jnp.bitwise_and(g, 3) - x), 3)
    came = onehot(2 * WIDE, offset * 2 + a_int).astype(F32)
    where_row[...] = jnp.concatenate([came, came], axis=0).astype(BF16)
    keep[...] = onehot(GROUP, r).astype(F32)
    line = lax.broadcasted_iota(I32, (MOST, MOST), 0)
    lane = lax.broadcasted_iota(I32, (MOST, MOST), 1)
    same = jnp.zeros((MOST, MOST), jnp.bool_)
    for b in range(MOST // SAMP):
        ends = (b * SAMP, (b + 1) * SAMP)
        same = jnp.logical_or(same, jnp.logical_and(jnp.logical_and(line >= ends[0], line < ends[1]),
                                                    jnp.logical_and(lane >= ends[0], lane < ends[1])))
    earlier[...] = jnp.logical_and(same, line < lane).astype(BF16)
    line = lax.broadcasted_iota(I32, (16, MOST), 0)
    lane = lax.broadcasted_iota(I32, (16, MOST), 1)
    pick[...] = jnp.logical_and(lane >= line * SAMP, lane < (line + 1) * SAMP).astype(BF16)

    for k in range(1, WIDE):
        metas[k].wait_recv()
        places[k].wait_recv()
    to_smem = pltpu.make_async_copy(pos_v, pos_s, local_sem.at[8])
    to_smem.start()
    flag = pos_v[0]
    for k in range(1, WIDE):
        flag = jnp.maximum(flag, pos_v[k])
    flag_s[...] = flag
    flags = {s: remote(flag_s, flag_r.at[s], flag_ss.at[s], flag_rs.at[s], narrow_at(s // 2, s % 2))
             for s in range(1, NARROW)}
    for copy in flags.values():
        copy.start()

    for s in (2, 6, 4):
        arrived(s, last)
        start(s + 1, last)
    own_weights[2].wait()
    for s in (1, 3, 7, 5):
        arrived(s, last)

    def spread(s, carry):
        lanes = lax.broadcasted_iota(I32, (REG * 4, 128), 1)
        line = lax.broadcasted_iota(I32, (REG * 4, 128), 0)
        channel = jnp.bitwise_and(line, 3)
        heads = wo[s].astype(F32).reshape(REG * 4, HID).astype(BF16)
        for j in range(REG):
            match = jnp.logical_and(jnp.right_shift(line, 2) == j, lanes == channel * GROUP + s * REG + j)
            wp[pl.ds((s * REG + j) * HID, HID)] = tn(heads, match.astype(BF16)).astype(BF16)
        return carry

    lax.fori_loop(0, NARROW, spread, 0)

    arrived(2, first), start(4, first), start(3, first)
    arrived(6, second), start(4, second), start(7, second)
    arrived(2, second), start(3, second)
    arrived(6, first), start(7, first)
    own_weights[0].wait(), own_weights[1].wait()
    for part in (first, second):
        arrived(1, part)
    to_smem.wait()

    returns = {}
    for q, chunk in enumerate(CHUNKS):
        size = len(chunk) * 2 * SAMP
        for k in chunk:
            if k:
                data_copy(k, 0, CAP).wait_recv()
        for order in HELD.get(q, ()):
            pack_all(order)
        acc[...] = jnp.zeros_like(acc)

        def regions(i, carry, q=q, chunk=chunk, size=size):
            dy = i + (i // 2) * (1 - 2 * (i % 2))
            if q == 0:
                @pl.when(i == 1)
                def _():
                    arrived(3, first), arrived(3, second)

                @pl.when(i == 2)
                def _():
                    arrived(4, first), start(5, first)
                    arrived(4, second), start(5, second)
                    arrived(7, first), arrived(7, second)

                @pl.when(i == 3)
                def _():
                    arrived(5, first), arrived(5, second)

            def rows_of(j):
                return jnp.concatenate(
                    [recv[q][s * CAP + within(pos_s[k, 0, ahead * GROUP + dy * 2 * REG + j], CAP)]
                     for s, k in enumerate(chunk) for ahead in range(2)], axis=0)

            span = range(2 * REG)
            hidden = [relu(dot(rows_of(j), wi[dy * 2 * REG + j])) for j in span]
            hidden = [relu(dot(hidden[j], wm[dy * 2 * REG + j, 0])) for j in span]
            hidden = [relu(dot(hidden[j], wm[dy * 2 * REG + j, 1])) for j in span]
            acc[0:size] += dot(jnp.concatenate(hidden, axis=1), wp[pl.ds(dy * 2 * REG * HID, 2 * REG * HID)])
            return carry

        lax.fori_loop(0, NARROW // 2, regions, 0)

        raw = acc[0:size].T
        gap = jnp.concatenate([meta_r[k, :, 0:2 * SAMP].astype(F32) for k in chunk], axis=1)
        density = raw[0:GROUP]
        density = jnp.maximum(density, 0.0) + jnp.log1p(jnp.exp(-jnp.abs(density)))
        optical = density * gap
        sums = dot(halves(optical), earlier[0:size, 0:size])
        passed = jnp.exp(-(sums[0:GROUP] + sums[GROUP:2 * GROUP]))
        series = optical * (1.0 - optical * (1 / 2 - optical * (1 / 6 - optical * (1 / 24 - optical * (1 / 120)))))
        weight = passed * jnp.where(optical < 0.125, series, 1.0 - jnp.exp(-optical))
        parts = [weight * jax.nn.sigmoid(raw[(c + 1) * GROUP:(c + 2) * GROUP]) for c in range(3)] + [optical]
        result = nt(pick[:, 0:size], halves(jnp.concatenate(parts, axis=0)))
        result = result[:, 0:128] + result[:, 128:256]
        for s, k in enumerate(chunk):
            target = ret_s if k else ret_r
            target[k] = result[2 * s:2 * s + 2]
            if k:
                returns[k] = remote(ret_s.at[k], ret_r.at[k], ret_ss.at[k], ret_rs.at[k], wide_at(k, -1))
                returns[k].start()

    for k in range(1, WIDE):
        returns[k].wait_recv()
    back = jnp.concatenate([ret_r[k] for k in range(WIDE)], axis=0)
    found = tn(halves(back), where_row[...])
    for c in range(4):
        fin_s[c:c + 1, :] = jnp.sum(found[c * GROUP:(c + 1) * GROUP] * keep[...], axis=0, keepdims=True)
    finals = {k: remote(fin_s, fin_r.at[wide], fin_ss.at[k], fin_rs.at[k], wide_at(k)) for k in range(1, WIDE)}
    for copy in finals.values():
        copy.start()
    fin_r[wide] = fin_s[...]
    for s in range(1, NARROW):
        flags[s].wait_recv()
        flag = jnp.maximum(flag, flag_r[s])
    over_out[...] = jnp.broadcast_to(flag[:, FLAG:FLAG + 1], (1, 128))
    for s in range(1, NARROW):
        for copy in weights[s]:
            copy.wait_send()
        flags[s].wait_send()
    for k in range(1, WIDE):
        metas[k].wait_send()
        places[k].wait_send()
        data_copy(k, 0, CAP).wait_send()
        returns[k].wait_send()
    for k in range(1, WIDE):
        remote(fin_s, fin_r.at[group_at(k, -1)], fin_ss.at[k], fin_rs.at[k], wide_at(k)).wait_recv()

    depth = [fin_r[s, 3:4, :] for s in range(WIDE)]
    ahead, behind = [jnp.zeros_like(depth[0])], [jnp.zeros_like(depth[0])]
    for s in range(WIDE - 1):
        ahead.append(ahead[-1] + depth[s])
        behind.append(behind[-1] + depth[WIDE - 1 - s])
    backward = dirs[...] == 1
    colour = jnp.zeros((3, ROWS), F32)
    for s in range(WIDE):
        light = jnp.exp(-jnp.where(backward, behind[WIDE - 1 - s], ahead[s]))
        colour = colour + light * fin_r[s, 0:3, :]
    out[...] = colour
    for k in range(1, WIDE):
        finals[k].wait_send()


def render(samples, spacing, ids, dirs, w_in, w_mid, w_out):
    vmem, smem, dma = pltpu.VMEM, pltpu.SMEM, pltpu.SemaphoreType.DMA
    regions = NARROW * REG
    whole, any_place = pl.BlockSpec(memory_space=pltpu.VMEM), pl.BlockSpec(memory_space=pl.ANY)
    scratch = [vmem((ROWS, SAMP, FEAT), BF16), vmem((WIDE - 1, CAP, SAMP, FEAT), BF16)]
    scratch += [vmem((len(chunk) * CAP, SAMP, FEAT), BF16) for chunk in CHUNKS]
    scratch += [
        vmem((regions, FEAT, HID), BF16), vmem((regions, 2, HID, HID), BF16), vmem((NARROW, REG, 4, HID), BF16),
        vmem((regions * HID, 128), BF16), vmem((WIDE, GROUP, 128), BF16), vmem((WIDE, GROUP, 128), BF16),
        vmem((WIDE, 1, 128), I32), vmem((WIDE, 1, 128), I32), smem((WIDE, 1, 128), I32), vmem((WIDE, 128), I32), smem((WIDE, 128), I32),
        vmem((MOST, 128), F32), vmem((MOST, MOST), BF16), vmem((16, MOST), BF16), vmem((4 * WIDE, ROWS), BF16),
        vmem((GROUP, ROWS), F32), vmem((WIDE, 2, 128), F32), vmem((WIDE, 2, 128), F32),
        vmem((4, ROWS), F32), vmem((WIDE, 4, ROWS), F32), vmem((1, 128), I32), vmem((NARROW, 1, 128), I32),
        dma((9,)), dma((5, NARROW)), dma((5, NARROW)), dma((WIDE,)), dma((WIDE,)), dma((WIDE,)), dma((WIDE,)), dma((WIDE,)),
        dma((WIDE,)), dma((WIDE,)), dma((WIDE,)), dma((WIDE,)), dma((WIDE,)), dma((NARROW,)), dma((NARROW,))]
    return pl.pallas_call(
        render_kernel,
        out_shape=(jax.ShapeDtypeStruct((3, ROWS), F32), jax.ShapeDtypeStruct((1, 128), I32)),
        in_specs=[any_place, whole, whole, whole, any_place, any_place, any_place],
        out_specs=(whole, whole),
        scratch_shapes=scratch,
        compiler_params=pltpu.CompilerParams(collective_id=0, has_side_effects=True, vmem_limit_bytes=58 * 2**20),
        name="render",
    )(samples, spacing, ids, dirs, w_in, w_mid, w_out)


def on_device(samples, spacing, region_ids, directions, w_in, w_mid, w_out):
    args = (samples, spacing, region_ids, directions, w_in, w_mid, w_out)
    fast, over = render(
        samples.reshape(ROWS, SAMP, FEAT), spacing.reshape(ROWS, SAMP).T, region_ids.reshape(1, ROWS),
        directions.reshape(1, ROWS), w_in, w_mid, w_out)
    return lax.cond(over[0, 0] > 0, lambda rest: general(*rest), lambda rest: fast, args)


def solution(mesh):
    in_specs = (
        P("wide", "narrow", None, None),
        P("wide", "narrow", None),
        P("wide", "narrow", None),
        P("narrow"),
        P(("wide", "narrow"), None, None),
        P(("wide", "narrow"), None, None, None),
        P(("wide", "narrow"), None, None),
    )
    out_specs = P(None, "narrow")
    return jax.shard_map(
        on_device, mesh=mesh, in_specs=in_specs, out_specs=out_specs, check_vma=False
    )
```
